256 devices in a mesh: dp: 16 (over z_lo, x, core), seq: 16 (over y, z_hi).
Axes of the slice: x: 4, y: 4, z: 8 (z_hi: 4, z_lo: 2; z = z_hi * 2 + z_lo), core: 2. Of those that a mesh axis runs over, the one named last changes fastest.
Arguments:
- queries: bfloat16 [16, 2048, 1536], P('dp', 'seq'), may hold values from -8 to 8
- keys: bfloat16 [16, 2048, 1536], P('dp', 'seq'), may hold values from -8 to 8
- values: bfloat16 [16, 2048, 1536], P('dp', 'seq'), may hold values from -12 to 12
- residual: bfloat16 [16, 2048, 1536], P('dp', 'seq'), may hold values from -6 to 6
- out_weight: bfloat16 [1536, 1536], P('seq'), may hold values from -0.15625 to 0.15625
- conv_weight: bfloat16 [5, 1536, 384], P(None, 'seq'), may hold values from -0.0625 to 0.0625
- skip: bfloat16 [16, 4096, 384], P('dp', 'seq'), may hold values from -6 to 6
- cotangent: bfloat16 [16, 4096, 384], P('dp', 'seq'), may hold values from -6 to 6
Outputs:
- decoded: bfloat16 [16, 4096, 384], P('dp', 'seq')
- grad_queries: bfloat16 [16, 2048, 1536], P('dp', 'seq')
- grad_keys: bfloat16 [16, 2048, 1536], P('dp', 'seq')
- grad_values: bfloat16 [16, 2048, 1536], P('dp', 'seq')
- grad_residual: bfloat16 [16, 2048, 1536], P('dp', 'seq')
- grad_out_weight: float32 [1536, 1536], P('seq')
- grad_conv_weight: float32 [5, 1536, 384], P(None, 'seq')
The draws below stay inside these ranges and needn't reach their ends.
All inputs are finite; a program needn't handle non-finite values.
Results may differ from the reference program's by a relative error of at most 0.029.
Values may be sent and summed in bfloat16 or wider, within the bound.
No kernel may reach another device: no remote copies, remote signals or barrier semaphores. Data moves between devices by JAX's collectives and lax.ppermute only.
A program may use at most 128 MiB of HBM per device.

```python
import math
import jax
import jax.numpy as jnp
from jax import lax

D = 1536
HEADS = 8
HEAD = 192
CHANNELS = 384
KERNEL = 5
TOK_DEV = 128
LENGTH = 2048
SEQS = 16
N_SEQ = 16


def draw_queries(key, part):
    key = jax.random.fold_in(key, 3)
    sampled = jnp.clip(1.5 * jax.random.normal(key, (SEQS, LENGTH, D), jnp.float32), -8.0, 8.0)
    return sampled.astype(jnp.bfloat16)


def draw_keys(key, part):
    key = jax.random.fold_in(key, 5)
    sampled = jnp.clip(1.5 * jax.random.normal(key, (SEQS, LENGTH, D), jnp.float32), -8.0, 8.0)
    return sampled.astype(jnp.bfloat16)


def spiked(values, stream_key, source, target, shards_of, factor):
    def block_of(dim):
        return (jnp.arange(values.shape[dim]) // (values.shape[dim] // shards_of)).reshape((-1,) + (1,) * (values.ndim - 1 - dim))

    first = jax.random.permutation(stream_key, shards_of)[block_of(target)]
    far = (block_of(target) + shards_of // 2) % shards_of
    return jnp.where((block_of(source) == first) | (block_of(source) == far), factor * values, values)


def steps_of(own_key, shape, shards, least, high):
    def one(axis_at, blocks):
        steps = jax.random.uniform(jax.random.fold_in(jax.random.fold_in(own_key, 6), axis_at), (blocks,), jnp.float32, least / len(shards), high / len(shards))
        return jnp.repeat(jnp.exp(steps), shape[axis_at] // blocks).reshape((-1,) + (1,) * (len(shape) - axis_at - 1))

    factor_of = one(*shards[0])
    for cut in shards[1:]:
        factor_of = factor_of * one(*cut)
    return factor_of


def scatter_about(rng, dims, spread, reach, cuts=(), kind=jnp.bfloat16):
    entries = spread * jax.random.normal(rng, dims, jnp.float32)
    if cuts:
        entries = entries * steps_of(rng, dims, cuts, -0.22, 0.18)
    return jnp.clip(entries, -reach, reach).astype(kind)


def bell_draw_with(own_key, shape, spread, reach, cuts, heavy, kind=jnp.bfloat16):
    array = spread * jax.random.normal(own_key, shape, jnp.float32)
    if cuts:
        array = array * steps_of(own_key, shape, cuts, -0.22, 0.18)
    return jnp.clip(spiked(array, jax.random.fold_in(own_key, 3), *heavy), -reach, reach).astype(kind)


def setup_inputs(seed: int = 0) -> dict:
    key_of = jax.random.split(jax.random.key(seed), 9)
    queries = draw_queries(jax.random.fold_in(key_of[8], 71), 0)
    keys = draw_keys(jax.random.fold_in(key_of[8], 71), 0)
    values = scatter_about(key_of[2], (SEQS, LENGTH, D), 3.0, 12.0, ((0, 16), (1, 16)))
    residual = bell_draw_with(key_of[3], (SEQS, LENGTH, D), 1.0, 6.0, ((0, 16), (1, 16)), (1, 2, 16, 2.0))
    out_weight = scatter_about(key_of[4], (D, D), D ** -0.5, 0.15625, ((0, 16),))
    conv_weight = scatter_about(key_of[5], (KERNEL, D, CHANNELS), (KERNEL * D) ** -0.5, 0.0625, ((1, 16),))
    skip = scatter_about(key_of[6], (SEQS, 2 * LENGTH, CHANNELS), 1.0, 6.0, ((0, 16), (1, 16)))
    cotangent = scatter_about(key_of[7], (SEQS, 2 * LENGTH, CHANNELS), 1.0, 6.0, ((0, 16), (1, 16)))
    return dict(queries=queries, keys=keys, values=values, residual=residual, out_weight=out_weight, conv_weight=conv_weight, skip=skip, cotangent=cotangent)


root_two_pi = math.sqrt(2.0 / math.pi)
cubic_term = 0.044715

def gelu_pair(pre_act):
    inner_arg = root_two_pi * (pre_act + cubic_term * pre_act * pre_act * pre_act)
    tanh_value = jnp.tanh(inner_arg)
    activated = 0.5 * pre_act * (1.0 + tanh_value)
    act_slope = 0.5 * (1.0 + tanh_value) + 0.5 * pre_act * (1.0 - tanh_value * tanh_value) * root_two_pi * (1.0 + 3.0 * cubic_term * pre_act * pre_act)
    return (activated, act_slope)

def round_trip(numbers):
    return lax.optimization_barrier(numbers.astype(jnp.bfloat16)).astype(jnp.float32)

def one_sequence(seq_queries, seq_keys, seq_values, seq_resid, seq_skip, seq_cotan, out_weight, conv_weight):
    score_scale = HEAD ** (-0.5)
    half_kernel = KERNEL // 2
    positions = 2 * LENGTH
    query_heads = seq_queries.reshape(LENGTH, HEADS, HEAD).astype(jnp.float32)
    key_heads = seq_keys.reshape(LENGTH, HEADS, HEAD).astype(jnp.float32)
    value_heads = seq_values.reshape(LENGTH, HEADS, HEAD).astype(jnp.float32)
    scores = jnp.einsum('qhd,khd->hqk', query_heads, key_heads) * score_scale
    row_peak = lax.optimization_barrier(jnp.max(scores, axis=2, keepdims=True))
    shifted_exp = jnp.exp(scores - row_peak)
    attn_probs = shifted_exp / lax.optimization_barrier(jnp.sum(shifted_exp, axis=2, keepdims=True))
    probs_low = round_trip(attn_probs)
    attended = jnp.einsum('hqk,khd->qhd', probs_low, value_heads).astype(jnp.bfloat16).reshape(LENGTH, D)
    mixed = (seq_resid.astype(jnp.float32) + jnp.dot(attended, out_weight, preferred_element_type=jnp.float32)).astype(jnp.bfloat16)
    upsampled = jnp.pad(jnp.repeat(mixed, 2, axis=0), ((half_kernel, half_kernel), (0, 0)))
    pre_act = jnp.zeros((positions, CHANNELS), jnp.float32)
    for tap_index in range(KERNEL):
        pre_act = pre_act + jnp.dot(upsampled[tap_index:tap_index + positions], conv_weight[tap_index], preferred_element_type=jnp.float32)
    activated, act_slope = gelu_pair(pre_act)
    decoded = (activated + seq_skip.astype(jnp.float32)).astype(jnp.bfloat16)
    grad_pre = (seq_cotan.astype(jnp.float32) * act_slope).astype(jnp.bfloat16)
    padded_grad = jnp.pad(grad_pre, ((half_kernel, half_kernel), (0, 0)))
    grad_up = jnp.zeros((positions, D), jnp.float32)
    for tap_index in range(KERNEL):
        first_row = 2 * half_kernel - tap_index
        grad_up = grad_up + jnp.dot(padded_grad[first_row:first_row + positions], conv_weight[tap_index].T, preferred_element_type=jnp.float32)
    grad_mixed = grad_up.reshape(LENGTH, 2, D).sum(axis=1).astype(jnp.bfloat16)
    grad_attended = jnp.dot(grad_mixed, out_weight.T, preferred_element_type=jnp.float32).astype(jnp.bfloat16)
    proj_terms = jnp.einsum('sti,stj->sij', attended.reshape(N_SEQ, TOK_DEV, D).astype(jnp.float32), grad_mixed.reshape(N_SEQ, TOK_DEV, D).astype(jnp.float32))
    grad_proj = lax.optimization_barrier(jnp.sum(round_trip(proj_terms), axis=0))
    slab_grad = grad_pre.reshape(N_SEQ, 2 * TOK_DEV, CHANNELS).astype(jnp.float32)
    conv_terms = []
    for tap_index in range(KERNEL):
        shifted_in = upsampled[tap_index:tap_index + positions].reshape(N_SEQ, 2 * TOK_DEV, D).astype(jnp.float32)
        conv_terms.append(lax.optimization_barrier(jnp.sum(round_trip(jnp.einsum('spd,spc->sdc', shifted_in, slab_grad)), axis=0)))
    grad_conv = jnp.stack(conv_terms)
    grad_heads = grad_attended.reshape(LENGTH, HEADS, HEAD).astype(jnp.float32)
    grad_probs = jnp.einsum('qhd,khd->hqk', grad_heads, value_heads)
    row_total = lax.optimization_barrier(jnp.sum(attn_probs * grad_probs, axis=2, keepdims=True))
    grad_scores = round_trip(attn_probs * (grad_probs - row_total) * score_scale)
    grad_queries = jnp.einsum('hqk,khd->qhd', grad_scores, key_heads).astype(jnp.bfloat16).reshape(LENGTH, D)
    grad_keys = jnp.einsum('hqk,qhd->khd', grad_scores, query_heads).astype(jnp.bfloat16).reshape(LENGTH, D)
    grad_values = jnp.einsum('hqk,qhd->khd', probs_low, grad_heads).astype(jnp.bfloat16).reshape(LENGTH, D)
    return (decoded, grad_queries, grad_keys, grad_values, grad_mixed, grad_proj, grad_conv)

def reference(queries, keys, values, residual, out_weight, conv_weight, skip, cotangent):

    def seq_step(running, batch_row):
        results = one_sequence(batch_row[0], batch_row[1], batch_row[2], batch_row[3], batch_row[4], batch_row[5], out_weight, conv_weight)
        return ((running[0] + results[5], running[1] + results[6]), (results[0], results[1], results[2], results[3], results[4]))
    zero_grads = (jnp.zeros((D, D), jnp.float32), jnp.zeros((KERNEL, D, CHANNELS), jnp.float32))
    totals, stacked = lax.scan(seq_step, zero_grads, (queries, keys, values, residual, skip, cotangent))
    return (stacked[0], stacked[1], stacked[2], stacked[3], stacked[4], totals[0], totals[1])
```

```python
import math

import jax
import jax.numpy as jnp
from jax import lax
from jax.experimental import pallas as pl
from jax.experimental.pallas import tpu as pltpu
from jax.sharding import Mesh
from jax.sharding import PartitionSpec as P

HEADS = 8
HEAD = 192
WIDTH = 1536
TOK = 128
HALF = 64
CH = 384
TAPS = 5
WCOLS = 768
CCOLS = 1024
TILE = 256
SEQ = ("y", "zh")
ROOT = math.sqrt(2.0 / math.pi)
CUBIC = 0.044715
SCALE = HEAD ** (-0.5)
SCALE2 = SCALE * math.log2(math.e)
BF = jnp.bfloat16
F32 = jnp.float32
VMEM = pl.BlockSpec(memory_space=pltpu.VMEM)
SMEM = pl.BlockSpec(memory_space=pltpu.SMEM)


def params():
    return pltpu.CompilerParams(vmem_limit_bytes=56 * 1024 * 1024)


def cost(flops, nbytes):
    return pl.CostEstimate(flops=int(flops), bytes_accessed=int(nbytes), transcendentals=0)


def shaped(shape, dtype=BF):
    return jax.ShapeDtypeStruct(shape, dtype)


def dot(a, b):
    return jnp.dot(a, b, preferred_element_type=F32)


def dot_nt(a, b):
    return lax.dot_general(a, b, (((1,), (1,)), ((), ())), preferred_element_type=F32)


def pack_kernel(q_ref, k_ref, v_ref, o_ref):
    for j, ref in enumerate((q_ref, k_ref, v_ref)):
        for half in range(2):
            for h in range(HEADS):
                o_ref[half, h, j] = ref[half * HALF : (half + 1) * HALF, h * HEAD : (h + 1) * HEAD]


def pack(q, k, v):
    return pl.pallas_call(
        pack_kernel,
        out_shape=shaped((2, HEADS, 3, HALF, HEAD)),
        in_specs=[VMEM] * 3,
        out_specs=VMEM,
        compiler_params=params(),
        cost_estimate=cost(0, 3 * 2 * TOK * WIDTH * 2),
    )(q, k, v)


def unpack_kernel(x_ref, q_ref, k_ref, v_ref):
    for j, ref in enumerate((q_ref, k_ref, v_ref)):
        for half in range(2):
            for h in range(HEADS):
                ref[half * HALF : (half + 1) * HALF, h * HEAD : (h + 1) * HEAD] = x_ref[half, h, j]


def unpack(x):
    return pl.pallas_call(
        unpack_kernel,
        out_shape=[shaped((TOK, WIDTH))] * 3,
        in_specs=[VMEM],
        out_specs=[VMEM] * 3,
        compiler_params=params(),
        cost_estimate=cost(0, 3 * 2 * TOK * WIDTH * 2),
    )(x)


def rows_of(ref, j):
    return ref[:, j].reshape(16 * HALF, HEAD)


def forward_kernel(mine_ref, other_ref, out_ref, lse_ref, vt_ref):
    step = pl.program_id(0)
    count = 16 * HALF

    @pl.when(step == 0)
    def _():
        vt_ref[:, :count] = rows_of(mine_ref, 2).T
        vt_ref[:, count:] = rows_of(other_ref, 2).T

    q = mine_ref[pl.ds(step * (TILE // HALF), TILE // HALF), 0].reshape(TILE, HEAD)
    s_a = dot_nt(rows_of(mine_ref, 1), q) * SCALE2
    s_b = dot_nt(rows_of(other_ref, 1), q) * SCALE2
    peak = jnp.maximum(jnp.max(s_a, axis=0, keepdims=True), jnp.max(s_b, axis=0, keepdims=True))
    e_a = jnp.exp2(s_a - peak)
    e_b = jnp.exp2(s_b - peak)
    total = jnp.sum(e_a, axis=0, keepdims=True) + jnp.sum(e_b, axis=0, keepdims=True)
    out = dot(vt_ref[:, :count], e_a.astype(BF)) + dot(vt_ref[:, count:], e_b.astype(BF))
    out = (out / total).T.astype(BF)
    out_ref[...] = out.reshape(TILE // HALF, HALF, HEAD)
    lse_ref[...] = peak + jnp.log2(total)


def attention_forward(mine, other):
    whole = pl.BlockSpec((16, 3, HALF, HEAD), lambda i: (0, 0, 0, 0))
    return pl.pallas_call(
        forward_kernel,
        grid=(16 * HALF // TILE,),
        out_shape=[shaped((16, HALF, HEAD)), shaped((1, 16 * HALF), F32)],
        in_specs=[whole, whole],
        out_specs=[
            pl.BlockSpec((TILE // HALF, HALF, HEAD), lambda i: (i, 0, 0)),
            pl.BlockSpec((1, TILE), lambda i: (0, i)),
        ],
        scratch_shapes=[pltpu.VMEM((HEAD, 32 * HALF), BF)],
        compiler_params=params(),
        cost_estimate=cost(4 * 1024 * 2048 * 256, 3 * 1024 * 1024),
    )(mine, other)


def backward_kernel(
    mine_ref, other_ref, out_ref, grad_ref, lse_ref, gq_ref, own_ref, far_ref, kt_ref, gk_ref, gv_ref
):
    step = pl.program_id(0)
    count = 16 * HALF

    @pl.when(step == 0)
    def _():
        kt_ref[:, :count] = rows_of(mine_ref, 1).T
        kt_ref[:, count:] = rows_of(other_ref, 1).T
        gk_ref[...] = jnp.zeros_like(gk_ref)
        gv_ref[...] = jnp.zeros_like(gv_ref)

    q = mine_ref[pl.ds(step * (TILE // HALF), TILE // HALF), 0].reshape(TILE, HEAD)
    grad = grad_ref[...].reshape(TILE, HEAD)
    out = out_ref[...].reshape(TILE, HEAD)
    delta = jnp.sum((grad.astype(F32) * out.astype(F32)).T, axis=0, keepdims=True)
    lse = lse_ref[...]
    gq = jnp.zeros((HEAD, TILE), F32)
    for part, ref in enumerate((mine_ref, other_ref)):
        span = slice(part * count, (part + 1) * count)
        probs = jnp.exp2(dot_nt(rows_of(ref, 1), q) * SCALE2 - lse)
        slope = (probs * (dot_nt(rows_of(ref, 2), grad) - delta)).astype(BF)
        gv_ref[span] += dot(probs.astype(BF), grad)
        gk_ref[span] += dot(slope, q)
        gq = gq + dot(kt_ref[:, span], slope)
    gq_ref[...] = (gq * SCALE).T.astype(BF).reshape(TILE // HALF, HALF, HEAD)

    @pl.when(step == pl.num_programs(0) - 1)
    def _():
        own_ref[:, 0] = (gk_ref[:count] * SCALE).reshape(16, HALF, HEAD)
        own_ref[:, 1] = gv_ref[:count].reshape(16, HALF, HEAD)
        far_ref[:, 0] = (gk_ref[count:] * SCALE).astype(BF).reshape(16, HALF, HEAD)
        far_ref[:, 1] = gv_ref[count:].astype(BF).reshape(16, HALF, HEAD)


def attention_backward(mine, other, out, grad, lse):
    whole = pl.BlockSpec((16, 3, HALF, HEAD), lambda i: (0, 0, 0, 0))
    part = pl.BlockSpec((TILE // HALF, HALF, HEAD), lambda i: (i, 0, 0))
    both = pl.BlockSpec((16, 2, HALF, HEAD), lambda i: (0, 0, 0, 0))
    return pl.pallas_call(
        backward_kernel,
        grid=(16 * HALF // TILE,),
        out_shape=[
            shaped((16, HALF, HEAD)),
            shaped((16, 2, HALF, HEAD), F32),
            shaped((16, 2, HALF, HEAD)),
        ],
        in_specs=[whole, whole, part, part, pl.BlockSpec((1, TILE), lambda i: (0, i))],
        out_specs=[part, both, both],
        scratch_shapes=[
            pltpu.VMEM((HEAD, 32 * HALF), BF),
            pltpu.VMEM((32 * HALF, HEAD), F32),
            pltpu.VMEM((32 * HALF, HEAD), F32),
        ],
        compiler_params=params(),
        cost_estimate=cost(10 * 1024 * 2048 * 256, 6 * 1024 * 1024),
    )(mine, other, out, grad, lse)


def row_index(shape):
    return lax.broadcasted_iota(jnp.int32, shape, 0)


def shifted_down(block, first):
    return jnp.where(row_index(block.shape) == 0, first, pltpu.roll(block, 1, 0))


def shifted_up(block, last):
    rows = block.shape[0]
    return jnp.where(row_index(block.shape) == rows - 1, last, pltpu.roll(block, rows - 1, 0))


OFFSETS = (0, 3, 1, 2)


def lanes(core, width):
    return pl.ds(pl.multiple_of(core * width, 128), width)


def up_kernel(at_ref, att_ref, res_ref, *refs):
    w_own, w_far = refs[:4], refs[4:8]
    c_own, c_far, mixed_ref, even_ref, odd_ref, fwd_ref, bwd_ref, acc_ref, y_ref = refs[8:]
    core, y = at_ref[0], at_ref[1]
    acc_ref[...] = res_ref[...].astype(F32)
    for k, off in enumerate(OFFSETS):
        head = 2 * lax.rem(y + off, 4)
        for j in range(2):
            block = att_ref[:, head + j].reshape(TOK, HEAD)
            rows = slice(j * HEAD, (j + 1) * HEAD)
            acc_ref[:, lanes(core, WCOLS)] += dot(block, w_own[k][rows])
            acc_ref[:, lanes(1 - core, WCOLS)] += dot(block, w_far[k][rows])
    mixed = acc_ref[...].astype(BF)
    mixed_ref[...] = mixed
    y_ref[:, lanes(core, CCOLS)] = dot(mixed, c_own[...])
    y_ref[:, lanes(1 - core, CCOLS)] = dot(mixed, c_far[...])
    y0, y1, y2, y3, y4 = (y_ref[:, t * CH : (t + 1) * CH] for t in range(TAPS))
    zero = jnp.zeros((1, CH), F32)
    low, high = y0 + y1, y3 + y4
    even_ref[...] = y2 + y3 + shifted_down(low, zero) + shifted_up(y4, zero)
    odd_ref[...] = y1 + y2 + shifted_down(y0, zero) + shifted_up(high, zero)
    fwd_ref[0:1] = low[TOK - 1 :]
    fwd_ref[1:2] = y0[TOK - 1 :]
    bwd_ref[0:1] = y4[:1]
    bwd_ref[1:2] = high[:1]


def project_up(at, att, residual, w_own, w_far, c_own, c_far):
    return pl.pallas_call(
        up_kernel,
        out_shape=[
            shaped((TOK, WIDTH)),
            shaped((TOK, CH), F32),
            shaped((TOK, CH), F32),
            shaped((2, CH), F32),
            shaped((2, CH), F32),
        ],
        in_specs=[SMEM] + [VMEM] * 12,
        out_specs=[VMEM] * 5,
        scratch_shapes=[pltpu.VMEM((TOK, WIDTH), F32), pltpu.VMEM((TOK, 2 * CCOLS), F32)],
        compiler_params=params(),
        cost_estimate=cost(2 * TOK * WIDTH * 3584, WIDTH * 3584 * 2),
    )(at, att, residual, *w_own, *w_far, c_own, c_far)


def gelu_kernel(even_ref, odd_ref, prev_ref, next_ref, skip_ref, cot_ref, dec_ref, gp_ref, first_ref, last_ref):
    for j, ref in enumerate((even_ref, odd_ref)):
        span = slice(j * CH, (j + 1) * CH)
        pre = ref[...]
        row = row_index(pre.shape)
        pre = pre + jnp.where(row == 0, prev_ref[j : j + 1], 0.0)
        pre = pre + jnp.where(row == TOK - 1, next_ref[j : j + 1], 0.0)
        tanh = jnp.tanh(ROOT * (pre + CUBIC * pre * pre * pre))
        act = 0.5 * pre * (1.0 + tanh)
        slope = 0.5 * (1.0 + tanh) + 0.5 * pre * (1.0 - tanh * tanh) * ROOT * (
            1.0 + 3.0 * CUBIC * pre * pre
        )
        dec_ref[:, span] = (act + skip_ref[:, span].astype(F32)).astype(BF)
        grad = (cot_ref[:, span].astype(F32) * slope).astype(BF)
        gp_ref[:, span] = grad
        wide = grad.astype(F32)
        first_ref[:, span] = wide[:1]
        last_ref[:, span] = wide[TOK - 1 :]


def gelu(even, odd, prev, nxt, skip, cot):
    return pl.pallas_call(
        gelu_kernel,
        out_shape=[
            shaped((TOK, 2 * CH)),
            shaped((TOK, 2 * CH)),
            shaped((1, 2 * CH), F32),
            shaped((1, 2 * CH), F32),
        ],
        in_specs=[VMEM] * 6,
        out_specs=[VMEM] * 4,
        compiler_params=params(),
        cost_estimate=cost(TOK * 768 * 30, TOK * 768 * 12),
    )(even, odd, prev, nxt, skip, cot)


def down_kernel(at_ref, gp_ref, prev_ref, next_ref, *refs):
    w_own, w_far = refs[:4], refs[4:8]
    c_own, c_far, gm_ref, gatt_ref, gm_keep, gm_send, g_keep, g_send, g_ref = refs[8:]
    core, y = at_ref[0], at_ref[1]
    e, o = gp_ref[:, :CH].astype(F32), gp_ref[:, CH:].astype(F32)
    e_up, o_up = shifted_up(e, next_ref[:, :CH]), shifted_up(o, next_ref[:, CH:])
    e_dn, o_dn = shifted_down(e, prev_ref[:, :CH]), shifted_down(o, prev_ref[:, CH:])
    for t, block in enumerate((e_up + o_up, o + e_up, e + o, o_dn + e, e_dn + o_dn)):
        g_ref[:, t * CH : (t + 1) * CH] = block.astype(BF)
    g_ref[:, TAPS * CH :] = jnp.zeros((TOK, 2 * CCOLS - TAPS * CH), BF)
    own, far = g_ref[:, lanes(core, CCOLS)], g_ref[:, lanes(1 - core, CCOLS)]
    g_keep[...] = own
    g_send[...] = far
    gm_ref[...] = (dot_nt(own, c_own[...]) + dot_nt(far, c_far[...])).astype(BF)
    own, far = gm_ref[:, lanes(core, WCOLS)], gm_ref[:, lanes(1 - core, WCOLS)]
    gm_keep[...] = own
    gm_send[...] = far
    for k, off in enumerate(OFFSETS):
        head = 2 * lax.rem(y + off, 4)
        for j in range(2):
            rows = slice(j * HEAD, (j + 1) * HEAD)
            block = dot_nt(own, w_own[k][rows]) + dot_nt(far, w_far[k][rows])
            gatt_ref[:, head + j] = block.astype(BF).reshape(2, HALF, HEAD)


def project_down(at, gp, prev, nxt, w_own, w_far, c_own, c_far):
    return pl.pallas_call(
        down_kernel,
        out_shape=[
            shaped((TOK, WIDTH)),
            shaped((2, HEADS, HALF, HEAD)),
            shaped((TOK, WCOLS)),
            shaped((TOK, WCOLS)),
            shaped((TOK, CCOLS)),
            shaped((TOK, CCOLS)),
        ],
        in_specs=[SMEM] + [VMEM] * 13,
        out_specs=[VMEM] * 6,
        scratch_shapes=[pltpu.VMEM((TOK, 2 * CCOLS), BF)],
        compiler_params=params(),
        cost_estimate=cost(2 * TOK * WIDTH * 3584, WIDTH * 3584 * 2),
    )(at, gp, prev, nxt, *w_own, *w_far, c_own, c_far)


def terms_kernel(a_ref, a2_ref, m_ref, m2_ref, gm_ref, gm2_ref, g_ref, g2_ref, o_ref):
    step = pl.program_id(0)
    for j in range(2):
        rows = slice(j * HEAD, (j + 1) * HEAD)
        a = a_ref[:, 2 * step + j].reshape(TOK, HEAD).T
        a2 = a2_ref[:, 2 * step + j].reshape(TOK, HEAD).T
        o_ref[rows, :WCOLS] = (dot(a, gm_ref[...]) + dot(a2, gm2_ref[...])).astype(BF)
    o_ref[:, WCOLS:] = (dot(m_ref[...].T, g_ref[...]) + dot(m2_ref[...].T, g2_ref[...])).astype(BF)


def weight_terms(att, att2, mixed, mixed2, gm, gm2, g, g2):
    heads = pl.BlockSpec((2, HEADS, HALF, HEAD), lambda i: (0, 0, 0, 0))
    cols = pl.BlockSpec((TOK, 2 * HEAD), lambda i: (0, i))
    gms = pl.BlockSpec((TOK, WCOLS), lambda i: (0, 0))
    gs = pl.BlockSpec((TOK, CCOLS), lambda i: (0, 0))
    return pl.pallas_call(
        terms_kernel,
        grid=(4,),
        out_shape=shaped((WIDTH, WCOLS + CCOLS)),
        in_specs=[heads, heads, cols, cols, gms, gms, gs, gs],
        out_specs=pl.BlockSpec((2 * HEAD, WCOLS + CCOLS), lambda i: (i, 0)),
        compiler_params=params(),
        cost_estimate=cost(4 * TOK * WIDTH * 1792, WIDTH * 1792 * 2),
    )(att, att2, mixed, mixed2, gm, gm2, g, g2)


def ring(axis, by, size=4):
    return [(i, (i + by) % size) for i in range(size)]


def swap(block, axis="core"):
    return lax.ppermute(block, axis, [(0, 1), (1, 0)])


def exchange(block, axis):
    return lax.all_to_all(block, axis, split_axis=0, concat_axis=0, tiled=True)


def neighbours(to_next, to_prev):
    up = [(i, i + 1) for i in range(15)]
    return (
        lax.ppermute(to_next, SEQ, up),
        lax.ppermute(to_prev, SEQ, [(b, a) for a, b in up]),
    )


def gathered_pieces(block):
    at = lax.axis_index("zh")
    later = [lax.ppermute(block, "zh", ring("zh", by)) for by in (3, 2, 1)]
    around = jnp.stack([block] + later + [block] + later[:2])
    piece = lax.dynamic_slice_in_dim(around, lax.rem(4 - at, 4), 4, axis=0)
    piece = piece.reshape(4 * block.shape[0], block.shape[1])
    return [piece] + [lax.ppermute(piece, "y", ring("y", (4 - off) % 4)) for off in OFFSETS[1:]]


def body(queries, keys, values, residual, out_weight, conv_weight, skip, cotangent):
    core = lax.axis_index("core")
    at = jnp.stack([core, lax.axis_index("y")]).astype(jnp.int32)

    conv_rows = jnp.pad(
        conv_weight.transpose(1, 0, 2).reshape(-1, TAPS * CH), ((0, 0), (0, 2 * CCOLS - TAPS * CH))
    )
    c_own = lax.all_gather(
        lax.dynamic_slice_in_dim(conv_rows, core * CCOLS, CCOLS, axis=1), SEQ, axis=0, tiled=True
    )
    w_own = gathered_pieces(lax.dynamic_slice_in_dim(out_weight, core * WCOLS, WCOLS, axis=1))
    w_far = [swap(piece) for piece in w_own]
    c_far = swap(c_own)

    packed = exchange(pack(queries[0], keys[0], values[0]), "core")
    mine = exchange(packed.reshape(16, 3, HALF, HEAD), SEQ)
    other = swap(mine)
    out, lse = attention_forward(mine, other)
    att = exchange(exchange(out, SEQ).reshape(2, HEADS, HALF, HEAD), "core")

    mixed, even, odd, to_next, to_prev = project_up(
        at, att, residual[0], w_own, w_far, c_own, c_far
    )
    prev, nxt = neighbours(to_next, to_prev)
    decoded, gp, first, last = gelu(
        even, odd, prev, nxt, skip[0].reshape(TOK, 2 * CH), cotangent[0].reshape(TOK, 2 * CH)
    )
    prev, nxt = neighbours(last, first)
    gm, gatt, gm_keep, gm_send, g_keep, g_send = project_down(
        at, gp, prev, nxt, w_own, w_far, c_own, c_far
    )

    term = weight_terms(
        att, swap(att), mixed, swap(mixed), gm_keep, swap(gm_send), g_keep, swap(g_send)
    )
    columns = WCOLS + CCOLS
    term = term.reshape(16, 4, 24, columns).transpose(1, 0, 2, 3).reshape(4 * 16 * 24, columns)
    part = lax.psum_scatter(term, "x", scatter_dimension=0, tiled=True)
    part = part.reshape(4, 4, 24, columns)
    part = jnp.sum(exchange(part, "y").astype(F32), axis=0).astype(BF)
    part = jnp.sum(exchange(part, "zh").astype(F32), axis=0).astype(BF)
    part = (part.astype(F32) + swap(part, "zl").astype(F32)).astype(BF)
    total = exchange(jnp.broadcast_to(part[None], (4, 24, columns)), "x").reshape(96, columns)

    grad = exchange(exchange(gatt, "core").reshape(16, HALF, HEAD), SEQ)
    gq, own, far = attention_backward(mine, other, out, grad, lse)
    both = (own + swap(far).astype(F32)).astype(BF)
    back = exchange(jnp.concatenate([gq[:, None], both], axis=1), SEQ)
    gq, gk, gv = unpack(exchange(back.reshape(2, HEADS, 3, HALF, HEAD), "core"))

    total_far = swap(total)
    low = jnp.where(core == 0, total, total_far)
    high = jnp.where(core == 0, total_far, total)
    grad_out = jnp.concatenate([low[:, :WCOLS], high[:, :WCOLS]], axis=1).astype(F32)
    grad_conv = jnp.concatenate([low[:, WCOLS:], high[:, WCOLS:]], axis=1)[:, : TAPS * CH]
    grad_conv = grad_conv.reshape(96, TAPS, CH).transpose(1, 0, 2).astype(F32)
    return (
        decoded.reshape(1, 2 * TOK, CH),
        gq[None],
        gk[None],
        gv[None],
        gm[None],
        grad_out,
        grad_conv,
    )


def solution(mesh):
    grid = Mesh(mesh.devices.reshape(2, 4, 2, 4, 4), ("zl", "x", "core", "y", "zh"))
    dp = ("zl", "x", "core")
    tokens = P(dp, SEQ, None)
    in_specs = (tokens, tokens, tokens, tokens, P(SEQ, None), P(None, SEQ, None), tokens, tokens)
    out_specs = (tokens, tokens, tokens, tokens, tokens, P(SEQ, None), P(None, SEQ, None))
    return jax.shard_map(body, mesh=grid, in_specs=in_specs, out_specs=out_specs, check_vma=False)
```

```python
import math

import jax
import jax.numpy as jnp
from jax import lax
from jax.experimental import pallas as pl
from jax.experimental.pallas import tpu as pltpu
from jax.sharding import Mesh
from jax.sharding import PartitionSpec as P

HEADS = 8
HEAD = 192
WIDTH = 1536
TOK = 128
HALF = 64
EDGE = 16
CH = 384
TAPS = 5
WCOLS = 768
CX = 256
CCOLS = 1024
TILE = 256
SEQ = ("y", "zh")
ROOT = math.sqrt(2.0 / math.pi)
CUBIC = 0.044715
SCALE = HEAD ** (-0.5)
SCALE2 = SCALE * math.log2(math.e)
BF = jnp.bfloat16
F32 = jnp.float32
VMEM = pl.BlockSpec(memory_space=pltpu.VMEM)
SMEM = pl.BlockSpec(memory_space=pltpu.SMEM)


def params():
    return pltpu.CompilerParams(vmem_limit_bytes=56 * 1024 * 1024)


def cost(flops, nbytes):
    return pl.CostEstimate(flops=int(flops) // 50, bytes_accessed=int(nbytes) // 50, transcendentals=0)


def shaped(shape, dtype=BF):
    return jax.ShapeDtypeStruct(shape, dtype)


def dot(a, b):
    return jnp.dot(a, b, preferred_element_type=F32)


def dot_nt(a, b):
    return lax.dot_general(a, b, (((1,), (1,)), ((), ())), preferred_element_type=F32)


def pack_kernel(q_ref, k_ref, v_ref, o_ref):
    for j, ref in enumerate((q_ref, k_ref, v_ref)):
        for half in range(2):
            for h in range(HEADS):
                o_ref[half, h, j] = ref[half * HALF : (half + 1) * HALF, h * HEAD : (h + 1) * HEAD]


def pack(q, k, v):
    return pl.pallas_call(
        pack_kernel,
        out_shape=shaped((2, HEADS, 3, HALF, HEAD)),
        in_specs=[VMEM] * 3,
        out_specs=VMEM,
        compiler_params=params(),
        cost_estimate=cost(0, 3 * 2 * TOK * WIDTH * 2),
    )(q, k, v)


def unpack_kernel(x_ref, q_ref, k_ref, v_ref):
    for j, ref in enumerate((q_ref, k_ref, v_ref)):
        for half in range(2):
            for h in range(HEADS):
                ref[half * HALF : (half + 1) * HALF, h * HEAD : (h + 1) * HEAD] = x_ref[half, h, j]


def unpack(x):
    return pl.pallas_call(
        unpack_kernel,
        out_shape=[shaped((TOK, WIDTH))] * 3,
        in_specs=[VMEM],
        out_specs=[VMEM] * 3,
        compiler_params=params(),
        cost_estimate=cost(0, 3 * 2 * TOK * WIDTH * 2),
    )(x)


def rows_of(ref, j):
    return ref[:, j].reshape(16 * HALF, HEAD)


def forward_kernel(at_ref, mine_ref, other_ref, out_ref, lse_ref, vt_ref):
    core, step = at_ref[0], pl.program_id(0)
    count = 16 * HALF

    @pl.when(step == 0)
    def _():
        vt_ref[:, :count] = rows_of(mine_ref, 2).T
        vt_ref[:, count:] = rows_of(other_ref, 2).T

    q = mine_ref[pl.ds(step * (TILE // HALF), TILE // HALF), 0].reshape(TILE, HEAD)
    s_a = dot_nt(rows_of(mine_ref, 1), q) * SCALE2
    s_b = dot_nt(rows_of(other_ref, 1), q) * SCALE2
    peak = jnp.maximum(jnp.max(s_a, axis=0, keepdims=True), jnp.max(s_b, axis=0, keepdims=True))
    e_a = jnp.exp2(s_a - peak)
    e_b = jnp.exp2(s_b - peak)
    total = jnp.sum(e_a, axis=0, keepdims=True) + jnp.sum(e_b, axis=0, keepdims=True)
    out = dot(vt_ref[:, :count], e_a.astype(BF)) + dot(vt_ref[:, count:], e_b.astype(BF))
    out = (out / total).T
    for j in range(TILE // HALF):
        slab = step * (TILE // HALF) + j
        rows = out[j * HALF : (j + 1) * HALF]
        out_ref[slab, :HALF] = rows.astype(BF)
        edge = jnp.where(core == 0, rows[:EDGE], rows[HALF - EDGE :])
        out_ref[lax.rem(slab + 15 + 2 * core, 16), HALF:] = edge.astype(BF)
    lse_ref[...] = peak + jnp.log2(total)


def attention_forward(at, mine, other):
    whole = pl.BlockSpec((16, 3, HALF, HEAD), lambda i: (0, 0, 0, 0))
    return pl.pallas_call(
        forward_kernel,
        grid=(16 * HALF // TILE,),
        out_shape=[shaped((16, HALF + EDGE, HEAD)), shaped((1, 16 * HALF), F32)],
        in_specs=[SMEM, whole, whole],
        out_specs=[
            pl.BlockSpec((16, HALF + EDGE, HEAD), lambda i: (0, 0, 0)),
            pl.BlockSpec((1, TILE), lambda i: (0, i)),
        ],
        scratch_shapes=[pltpu.VMEM((HEAD, 32 * HALF), BF)],
        compiler_params=params(),
        cost_estimate=cost(4 * 1024 * 2048 * 256, 3 * 1024 * 1024),
    )(at, mine, other)


def backward_kernel(
    mine_ref, other_ref, out_ref, grad_ref, lse_ref, gq_ref, own_ref, far_ref, kt_ref, gk_ref, gv_ref
):
    step = pl.program_id(0)
    count = 16 * HALF

    @pl.when(step == 0)
    def _():
        kt_ref[:, :count] = rows_of(mine_ref, 1).T
        kt_ref[:, count:] = rows_of(other_ref, 1).T
        gk_ref[...] = jnp.zeros_like(gk_ref)
        gv_ref[...] = jnp.zeros_like(gv_ref)

    q = mine_ref[pl.ds(step * (TILE // HALF), TILE // HALF), 0].reshape(TILE, HEAD)
    grad = grad_ref[...].reshape(TILE, HEAD)
    out = out_ref[:, :HALF].reshape(TILE, HEAD)
    delta = jnp.sum((grad.astype(F32) * out.astype(F32)).T, axis=0, keepdims=True)
    lse = lse_ref[...]
    gq = jnp.zeros((HEAD, TILE), F32)
    for part, ref in enumerate((mine_ref, other_ref)):
        span = slice(part * count, (part + 1) * count)
        probs = jnp.exp2(dot_nt(rows_of(ref, 1), q) * SCALE2 - lse)
        slope = (probs * (dot_nt(rows_of(ref, 2), grad) - delta)).astype(BF)
        gv_ref[span] += dot(probs.astype(BF), grad)
        gk_ref[span] += dot(slope, q)
        gq = gq + dot(kt_ref[:, span], slope)
    gq_ref[...] = (gq * SCALE).T.astype(BF).reshape(TILE // HALF, HALF, HEAD)

    @pl.when(step == pl.num_programs(0) - 1)
    def _():
        own_ref[:, 0] = (gk_ref[:count] * SCALE).astype(BF).reshape(16, HALF, HEAD)
        own_ref[:, 1] = gv_ref[:count].astype(BF).reshape(16, HALF, HEAD)
        far_ref[:, 0] = (gk_ref[count:] * SCALE).astype(BF).reshape(16, HALF, HEAD)
        far_ref[:, 1] = gv_ref[count:].astype(BF).reshape(16, HALF, HEAD)


def attention_backward(mine, other, out, grad, lse):
    whole = pl.BlockSpec((16, 3, HALF, HEAD), lambda i: (0, 0, 0, 0))
    part = pl.BlockSpec((TILE // HALF, HALF, HEAD), lambda i: (i, 0, 0))
    wide = pl.BlockSpec((TILE // HALF, HALF + EDGE, HEAD), lambda i: (i, 0, 0))
    both = pl.BlockSpec((16, 2, HALF, HEAD), lambda i: (0, 0, 0, 0))
    return pl.pallas_call(
        backward_kernel,
        grid=(16 * HALF // TILE,),
        out_shape=[
            shaped((16, HALF, HEAD)),
            shaped((16, 2, HALF, HEAD)),
            shaped((16, 2, HALF, HEAD)),
        ],
        in_specs=[whole, whole, wide, part, pl.BlockSpec((1, TILE), lambda i: (0, i))],
        out_specs=[part, both, both],
        scratch_shapes=[
            pltpu.VMEM((HEAD, 32 * HALF), BF),
            pltpu.VMEM((32 * HALF, HEAD), F32),
            pltpu.VMEM((32 * HALF, HEAD), F32),
        ],
        compiler_params=params(),
        cost_estimate=cost(10 * 1024 * 2048 * 256, 6 * 1024 * 1024),
    )(mine, other, out, grad, lse)


def row_index(shape):
    return lax.broadcasted_iota(jnp.int32, shape, 0)


def earlier(block):
    return pltpu.roll(block, 1, 0)


def later(block):
    return pltpu.roll(block, block.shape[0] - 1, 0)


def lanes(core, width):
    return pl.ds(pl.multiple_of(core * width, 128), width)


def offset(start, by, width):
    return pl.ds(pl.multiple_of(start + by * width, 128), width)


def middle_kernel(at_ref, att_ref, res_ref, cot_ref, lo_ref, hi_ref, skip_ref, w_own, w_far, *refs):
    c_own, c_far = refs[:4], refs[4:8]
    dec_ref, mixed_ref, g_keep, g_send, gm_ref, gm_keep, gm_send, gatt_ref = refs[8:16]
    acc_ref, y_ref, m_ref, g_ref = refs[16:]
    core, x, slab = at_ref[0], at_ref[1], at_ref[2]
    inside = slice(EDGE, EDGE + TOK)

    low = high = None
    for h in range(HEADS):
        block = jnp.concatenate(
            [att_ref[1, h, HALF:], att_ref[0, h, :HALF], att_ref[1, h, :HALF], att_ref[0, h, HALF:]],
            axis=0,
        )
        a = dot(block, w_own[h * HEAD : (h + 1) * HEAD])
        b = dot(block, w_far[h * HEAD : (h + 1) * HEAD])
        low, high = (a, b) if low is None else (low + a, high + b)
    acc_ref[:, lanes(core, WCOLS)] = low
    acc_ref[:, lanes(1 - core, WCOLS)] = high
    res = jnp.concatenate([lo_ref[:, :WIDTH], res_ref[...], hi_ref[:, :WIDTH]], axis=0)
    mixed = acc_ref[...] + res.astype(F32)
    row = row_index(mixed.shape)
    outside = ((row < EDGE) & (slab == 0)) | ((row >= EDGE + TOK) & (slab == 15))
    m_ref[...] = jnp.where(outside, 0.0, mixed).astype(BF)
    mixed_ref[...] = m_ref[inside]

    for k in range(4):
        by = lax.rem(x + k, 4)
        y_ref[:, offset(core * CCOLS, by, CX)] = dot(m_ref[...], c_own[k][...])
        y_ref[:, offset((1 - core) * CCOLS, by, CX)] = dot(m_ref[...], c_far[k][...])
    y0, y1, y2, y3, y4 = (y_ref[:, t * CH : (t + 1) * CH] for t in range(TAPS))
    even = y2 + y3 + earlier(y0 + y1) + later(y4)
    odd = y1 + y2 + earlier(y0) + later(y3 + y4)
    cot = jnp.concatenate([lo_ref[:, WIDTH:], cot_ref[...], hi_ref[:, WIDTH:]], axis=0)
    grads = []
    for j, pre in enumerate((even, odd)):
        span = slice(j * CH, (j + 1) * CH)
        tanh = jnp.tanh(ROOT * (pre + CUBIC * pre * pre * pre))
        act = 0.5 * pre * (1.0 + tanh)
        slope = 0.5 * (1.0 + tanh) + 0.5 * pre * (1.0 - tanh * tanh) * ROOT * (
            1.0 + 3.0 * CUBIC * pre * pre
        )
        dec_ref[:, span] = (act[inside] + skip_ref[:, span].astype(F32)).astype(BF)
        grads.append((cot[:, span].astype(F32) * slope).astype(BF).astype(F32))

    e, o = grads
    sums = (later(e) + later(o), o + later(e), e + o, earlier(o) + e, earlier(e) + earlier(o))
    for t, block in enumerate(sums):
        g_ref[:, t * CH : (t + 1) * CH] = block[inside].astype(BF)
    g_ref[:, TAPS * CH :] = jnp.zeros((TOK, 2 * CCOLS - TAPS * CH), BF)
    g_keep[...] = g_ref[:, lanes(core, CCOLS)]
    g_send[...] = g_ref[:, lanes(1 - core, CCOLS)]
    gm = jnp.zeros((TOK, WIDTH), F32)
    for k in range(4):
        lanes_k = offset(0, lax.rem(x + k, 4), CX)
        gm = gm + dot_nt(g_keep[:, lanes_k], c_own[k][...]) + dot_nt(g_send[:, lanes_k], c_far[k][...])
    gm_ref[...] = gm.astype(BF)
    gm_keep[...] = gm_ref[:, lanes(core, WCOLS)]
    gm_send[...] = gm_ref[:, lanes(1 - core, WCOLS)]
    for h in range(HEADS):
        rows = slice(h * HEAD, (h + 1) * HEAD)
        block = dot_nt(gm_keep[...], w_own[rows]) + dot_nt(gm_send[...], w_far[rows])
        gatt_ref[:, h] = block.astype(BF).reshape(2, HALF, HEAD)


def middle(at, att, residual, cotangent, edges, skip, weights):
    rows = TOK + 2 * EDGE
    return pl.pallas_call(
        middle_kernel,
        out_shape=[
            shaped((TOK, 2 * CH)),
            shaped((TOK, WIDTH)),
            shaped((TOK, CCOLS)),
            shaped((TOK, CCOLS)),
            shaped((TOK, WIDTH)),
            shaped((TOK, WCOLS)),
            shaped((TOK, WCOLS)),
            shaped((2, HEADS, HALF, HEAD)),
        ],
        in_specs=[SMEM] + [VMEM] * (6 + len(weights)),
        out_specs=[VMEM] * 8,
        scratch_shapes=[
            pltpu.VMEM((rows, WIDTH), F32),
            pltpu.VMEM((rows, 2 * CCOLS), F32),
            pltpu.VMEM((rows, WIDTH), BF),
            pltpu.VMEM((TOK, 2 * CCOLS), BF),
        ],
        compiler_params=params(),
        cost_estimate=cost(8 * rows * WIDTH * 3584, WIDTH * 3584 * 2),
    )(at, att, residual, cotangent, *edges, skip, *weights)


def conv_terms_kernel(m_ref, m2_ref, g_ref, g2_ref, out_ref, turned):
    turned[:, :TOK] = m_ref[...].astype(F32).T
    turned[:, TOK:] = m2_ref[...].astype(F32).T
    for x in range(4):
        rows = [turned[z * 96 + x * 24 : z * 96 + (x + 1) * 24] for z in range(4)]
        rows = jnp.concatenate(rows, axis=0).astype(BF)
        block = dot(rows[:, :TOK], g_ref[...]) + dot(rows[:, TOK:], g2_ref[...])
        out_ref[x] = block.astype(BF)


def conv_terms(mixed, mixed2, g, g2):
    cols = pl.BlockSpec((TOK, 2 * HEAD), lambda i: (0, i))
    gs = pl.BlockSpec((TOK, CCOLS), lambda i: (0, 0))
    return pl.pallas_call(
        conv_terms_kernel,
        grid=(4,),
        out_shape=shaped((4, 16 * 24, CCOLS)),
        in_specs=[cols, cols, gs, gs],
        out_specs=pl.BlockSpec((4, 4 * 24, CCOLS), lambda i: (0, i, 0)),
        scratch_shapes=[pltpu.VMEM((2 * HEAD, 2 * TOK), F32)],
        compiler_params=params(),
        cost_estimate=cost(4 * TOK * WIDTH * CCOLS, WIDTH * CCOLS * 2),
    )(mixed, mixed2, g, g2)


def proj_terms_kernel(y_ref, a_ref, a2_ref, gm_ref, gm2_ref, *out_refs):
    for k, ref in enumerate(out_refs):
        head = 2 * lax.rem(y_ref[0] + k, 4)
        for j in range(2):
            a = a_ref[:, head + j, :HALF].reshape(TOK, HEAD).T
            a2 = a2_ref[:, head + j, :HALF].reshape(TOK, HEAD).T
            block = dot(a, gm_ref[...]) + dot(a2, gm2_ref[...])
            ref[j * HEAD : (j + 1) * HEAD] = block.astype(BF)


def proj_terms(y, att, att2, gm, gm2):
    return pl.pallas_call(
        proj_terms_kernel,
        out_shape=[shaped((2 * HEAD, WCOLS))] * 4,
        in_specs=[SMEM] + [VMEM] * 4,
        out_specs=[VMEM] * 4,
        compiler_params=params(),
        cost_estimate=cost(4 * TOK * WIDTH * WCOLS, WIDTH * WCOLS * 2),
    )(y, att, att2, gm, gm2)


def place_kernel(at_ref, *refs):
    out_ref = refs[-1]
    for k, ref in enumerate(refs[:-1]):
        count = ref.shape[0]
        spot = lax.rem(at_ref[0] + k, 4)
        out_ref[pl.ds(pl.multiple_of(spot * count, 16), count)] = ref[...]


def place(at, pieces):
    rows, columns = pieces[0].shape
    return pl.pallas_call(
        place_kernel,
        out_shape=shaped((4 * rows, columns)),
        in_specs=[SMEM] + [VMEM] * 4,
        out_specs=VMEM,
        compiler_params=params(),
        cost_estimate=cost(0, 16 * rows * columns),
    )(at[None], *pieces)


def merge_kernel(gq_ref, own_ref, far_ref, out_ref):
    out_ref[:, 0] = gq_ref[...]
    out_ref[:, 1:] = (own_ref[...].astype(F32) + far_ref[...].astype(F32)).astype(BF)


def merge(gq, own, far):
    return pl.pallas_call(
        merge_kernel,
        out_shape=shaped((16, 3, HALF, HEAD)),
        in_specs=[VMEM] * 3,
        out_specs=VMEM,
        compiler_params=params(),
        cost_estimate=cost(0, 16 * HALF * HEAD * 18),
    )(gq, own, far)


def finish_kernel(at_ref, *refs):
    pieces = refs[:4]
    out_ref, conv_ref, scratch = refs[4:]
    core, x = at_ref[0], at_ref[1]
    far = 1 - core
    columns = WCOLS + CCOLS
    for k, ref in enumerate(pieces):
        rows = pl.ds(pl.multiple_of(lax.rem(x + k, 4) * 24, 8), 24)
        block = ref[...].astype(F32)
        out_ref[rows, lanes(core, WCOLS)] = block[:, :WCOLS]
        out_ref[rows, lanes(far, WCOLS)] = block[:, columns : columns + WCOLS]
        scratch[:, lanes(core, CCOLS)] = block[:, WCOLS:columns]
        scratch[:, lanes(far, CCOLS)] = block[:, columns + WCOLS :]
        for t in range(TAPS):
            conv_ref[t, rows] = scratch[:, t * CH : (t + 1) * CH]


def finish(at, pieces):
    return pl.pallas_call(
        finish_kernel,
        out_shape=[shaped((96, WIDTH), F32), shaped((TAPS, 96, CH), F32)],
        in_specs=[SMEM] + [VMEM] * 4,
        out_specs=[VMEM] * 2,
        scratch_shapes=[pltpu.VMEM((24, 2 * CCOLS), F32)],
        compiler_params=params(),
        cost_estimate=cost(0, 96 * 3584 * 6),
    )(at, *pieces)


def tied(block, *others):
    return lax.optimization_barrier((block, *others))[0]


def shifted(block, axis, by):
    return lax.ppermute(block, axis, [((i + by) % 4, i) for i in range(4)])


def around(block, axis):
    return [block] + [shifted(block, axis, by) for by in (1, 2, 3)]


def sent_to(parts, axis):
    return [parts[0]] + [shifted(parts[k], axis, 4 - k) for k in (1, 2, 3)]


def parts_of(blocks, axis, dim=0):
    at = lax.axis_index(axis)
    return [
        lax.dynamic_index_in_dim(blocks, lax.rem(at + k, 4), dim, keepdims=False) for k in range(4)
    ]


def summed(blocks):
    total = blocks[0].astype(F32)
    for block in blocks[1:]:
        total = total + block.astype(F32)
    return total.astype(BF)


def swap(block, axis="core"):
    return lax.ppermute(block, axis, [(0, 1), (1, 0)])


def exchange(block, axis):
    return lax.all_to_all(block, axis, split_axis=0, concat_axis=0, tiled=True)


def neighbours(to_next, to_prev):
    up = [(i, i + 1) for i in range(15)]
    return (
        lax.ppermute(to_next, SEQ, up),
        lax.ppermute(to_prev, SEQ, [(b, a) for a, b in up]),
    )


def body(queries, keys, values, residual, out_weight, conv_weight, skip, cotangent):
    core, x, y, zh = (lax.axis_index(a).astype(jnp.int32) for a in ("core", "x", "y", "zh"))
    at = jnp.stack([core, x, 4 * y + zh])
    residual, cotangent = residual[0], cotangent[0].reshape(TOK, 2 * CH)
    edges = [
        jnp.concatenate([block[rows] for block in (residual, cotangent)], axis=1)
        for rows in (slice(-EDGE, None), slice(0, EDGE))
    ]

    conv_rows = jnp.pad(
        conv_weight.transpose(1, 0, 2).reshape(-1, TAPS * CH), ((0, 0), (0, 2 * CCOLS - TAPS * CH))
    )
    c_part = lax.dynamic_slice_in_dim(conv_rows, core * CCOLS + x * CX, CX, axis=1)
    c_part = place(zh, around(c_part, "zh"))
    w_own = lax.dynamic_slice_in_dim(out_weight, core * WCOLS, WCOLS, axis=1)
    w_own = lax.all_gather(w_own, SEQ, axis=0, tiled=True)

    packed = exchange(pack(queries[0], keys[0], values[0]), "core")
    mine = exchange(tied(packed, c_part).reshape(16, 3, HALF, HEAD), SEQ)
    c_all = place(y, around(c_part, "y"))
    c_own, edges = around(c_all, "x"), neighbours(*edges)
    mine = tied(mine, c_own[1], c_own[3], *edges)
    other = swap(mine)
    out, lse = attention_forward(at, mine, other)
    back = exchange(out, SEQ)
    w_own = tied(w_own, out)
    w_far = swap(w_own)
    c_far = [swap(tied(piece, out)) for piece in c_own]
    att = exchange(back.reshape(2, HEADS, HALF + EDGE, HEAD), "core")

    weights = [w_own, w_far, *c_own, *c_far]
    skip = skip[0].reshape(TOK, 2 * CH)
    decoded, mixed, g_keep, g_send, gm, gm_keep, gm_send, gatt = middle(
        at, att, residual, cotangent, edges, skip, weights
    )

    proj = proj_terms(y[None], att, swap(att), gm_keep, swap(gm_send))
    conv = conv_terms(mixed, swap(mixed), g_keep, swap(g_send))
    gatt = tied(exchange(gatt, "core"), conv, proj[0])
    conv = lax.psum_scatter(conv.reshape(-1, CCOLS), "x", scatter_dimension=0, tiled=True)
    proj = sent_to(proj, "y")

    grad = tied(exchange(gatt.reshape(16, HALF, HEAD), SEQ), proj[0])
    gq, own, far = attention_backward(mine, other, out, grad, lse)
    both = merge(gq, own, swap(tied(far, *proj)))
    conv = parts_of(tied(conv, both).reshape(4, 96, CCOLS), "y")
    proj = summed([tied(b, both) for b in proj]).reshape(4, 4, 24, WCOLS)
    proj = [b.reshape(96, WCOLS) for b in parts_of(proj, "x", 1)]
    conv, proj = summed(sent_to(conv, "y")), summed(sent_to(proj, "x"))
    part = jnp.concatenate([proj, conv], axis=1).reshape(4, 24, WCOLS + CCOLS)
    part = sent_to(parts_of(part, "zh"), "zh")
    back = exchange(both, SEQ)

    part = summed([tied(b, back) for b in part])
    part = (part.astype(F32) + swap(part, "zl").astype(F32)).astype(BF)
    gq, gk, gv = unpack(exchange(back.reshape(2, HEADS, 3, HALF, HEAD), "core"))
    pieces = around(tied(jnp.concatenate([part, swap(part)], axis=1), gq), "x")
    grad_out, grad_conv = finish(jnp.stack([core, x]), pieces)
    return (
        decoded.reshape(1, 2 * TOK, CH),
        gq[None],
        gk[None],
        gv[None],
        gm[None],
        grad_out,
        grad_conv,
    )


def solution(mesh):
    grid = Mesh(mesh.devices.reshape(2, 4, 2, 4, 4), ("zl", "x", "core", "y", "zh"))
    dp = ("zl", "x", "core")
    tokens = P(dp, SEQ, None)
    in_specs = (tokens, tokens, tokens, tokens, P(SEQ, None), P(None, SEQ, None), tokens, tokens)
    out_specs = (tokens, tokens, tokens, tokens, tokens, P(SEQ, None), P(None, SEQ, None))
    return jax.shard_map(body, mesh=grid, in_specs=in_specs, out_specs=out_specs, check_vma=False)
```

```python
import math

import jax
import jax.numpy as jnp
from jax import lax
from jax.experimental import pallas as pl
from jax.experimental.pallas import tpu as pltpu
from jax.sharding import Mesh
from jax.sharding import PartitionSpec as P

HEADS = 8
HEAD = 192
WIDTH = 1536
TOK = 128
HALF = 64
EDGE = 16
CH = 384
TAPS = 5
WCOLS = 768
CX = 256
CCOLS = 1024
TILE = 256
SEQ = ("y", "zh")
ROOT = math.sqrt(2.0 / math.pi)
CUBIC = 0.044715
SCALE = HEAD ** (-0.5)
SCALE2 = SCALE * math.log2(math.e)
BF = jnp.bfloat16
F32 = jnp.float32
VMEM = pl.BlockSpec(memory_space=pltpu.VMEM)
SMEM = pl.BlockSpec(memory_space=pltpu.SMEM)


def params():
    return pltpu.CompilerParams(vmem_limit_bytes=56 * 1024 * 1024)


def cost(flops, nbytes):
    return pl.CostEstimate(flops=int(flops) // 50, bytes_accessed=int(nbytes) // 50, transcendentals=0)


def shaped(shape, dtype=BF):
    return jax.ShapeDtypeStruct(shape, dtype)


def dot(a, b):
    return jnp.dot(a, b, preferred_element_type=F32)


def dot_nt(a, b):
    return lax.dot_general(a, b, (((1,), (1,)), ((), ())), preferred_element_type=F32)


def pack_kernel(q_ref, k_ref, v_ref, o_ref):
    for j, ref in enumerate((q_ref, k_ref, v_ref)):
        for half in range(2):
            for h in range(HEADS):
                o_ref[half, h, j] = ref[half * HALF : (half + 1) * HALF, h * HEAD : (h + 1) * HEAD]


def pack(q, k, v):
    return pl.pallas_call(
        pack_kernel,
        out_shape=shaped((2, HEADS, 3, HALF, HEAD)),
        in_specs=[VMEM] * 3,
        out_specs=VMEM,
        compiler_params=params(),
        cost_estimate=cost(0, 3 * 2 * TOK * WIDTH * 2),
    )(q, k, v)


def unpack_kernel(at_ref, keep_ref, far_ref, q_ref, k_ref, v_ref):
    core = at_ref[0]
    for j, ref in enumerate((q_ref, k_ref, v_ref)):
        for h in range(HEADS):
            lanes_h = slice(h * HEAD, (h + 1) * HEAD)
            ref[pl.ds(pl.multiple_of(core * HALF, HALF), HALF), lanes_h] = keep_ref[h, j]
            ref[pl.ds(pl.multiple_of((1 - core) * HALF, HALF), HALF), lanes_h] = far_ref[h, j]


def unpack(at, keep, far):
    return pl.pallas_call(
        unpack_kernel,
        out_shape=[shaped((TOK, WIDTH))] * 3,
        in_specs=[SMEM] + [VMEM] * 2,
        out_specs=[VMEM] * 3,
        compiler_params=params(),
        cost_estimate=cost(0, 3 * 2 * TOK * WIDTH * 2),
    )(at, keep, far)


def join_kernel(at_ref, own_ref, far_ref, out_ref):
    core = at_ref[0]
    out_ref[pl.ds(core * HEADS, HEADS)] = own_ref[...]
    out_ref[pl.ds((1 - core) * HEADS, HEADS)] = far_ref[...]


def join(at, own, far):
    return pl.pallas_call(
        join_kernel,
        out_shape=shaped((2 * own.shape[0], *own.shape[1:])),
        in_specs=[SMEM] + [VMEM] * 2,
        out_specs=VMEM,
        compiler_params=params(),
        cost_estimate=cost(0, own.size * 8),
    )(at, own, far)


def rows_of(ref, j):
    return ref[:, j].reshape(16 * HALF, HEAD)


def forward_kernel(at_ref, mine_ref, other_ref, out_ref, lse_ref, vt_ref):
    core, step = at_ref[0], pl.program_id(0)
    count = 16 * HALF

    @pl.when(step == 0)
    def _():
        vt_ref[:, :count] = rows_of(mine_ref, 2).T
        vt_ref[:, count:] = rows_of(other_ref, 2).T

    q = mine_ref[pl.ds(step * (TILE // HALF), TILE // HALF), 0].reshape(TILE, HEAD)
    s_a = dot_nt(rows_of(mine_ref, 1), q) * SCALE2
    s_b = dot_nt(rows_of(other_ref, 1), q) * SCALE2
    peak = jnp.maximum(jnp.max(s_a, axis=0, keepdims=True), jnp.max(s_b, axis=0, keepdims=True))
    e_a = jnp.exp2(s_a - peak)
    e_b = jnp.exp2(s_b - peak)
    total = jnp.sum(e_a, axis=0, keepdims=True) + jnp.sum(e_b, axis=0, keepdims=True)
    out = dot(vt_ref[:, :count], e_a.astype(BF)) + dot(vt_ref[:, count:], e_b.astype(BF))
    out = (out / total).T
    for j in range(TILE // HALF):
        slab = step * (TILE // HALF) + j
        rows = out[j * HALF : (j + 1) * HALF]
        out_ref[slab, :HALF] = rows.astype(BF)
        edge = jnp.where(core == 0, rows[:EDGE], rows[HALF - EDGE :])
        out_ref[lax.rem(slab + 15 + 2 * core, 16), HALF:] = edge.astype(BF)
    lse_ref[...] = peak + jnp.log2(total)


def attention_forward(at, mine, other):
    whole = pl.BlockSpec((16, 3, HALF, HEAD), lambda i: (0, 0, 0, 0))
    return pl.pallas_call(
        forward_kernel,
        grid=(16 * HALF // TILE,),
        out_shape=[shaped((16, HALF + EDGE, HEAD)), shaped((1, 16 * HALF), F32)],
        in_specs=[SMEM, whole, whole],
        out_specs=[
            pl.BlockSpec((16, HALF + EDGE, HEAD), lambda i: (0, 0, 0)),
            pl.BlockSpec((1, TILE), lambda i: (0, i)),
        ],
        scratch_shapes=[pltpu.VMEM((HEAD, 32 * HALF), BF)],
        compiler_params=params(),
        cost_estimate=cost(4 * 1024 * 2048 * 256, 3 * 1024 * 1024),
    )(at, mine, other)


def backward_kernel(
    mine_ref, other_ref, out_ref, grad_ref, lse_ref, gq_ref, own_ref, far_ref, kt_ref, gk_ref, gv_ref
):
    step = pl.program_id(0)
    count = 16 * HALF

    @pl.when(step == 0)
    def _():
        kt_ref[:, :count] = rows_of(mine_ref, 1).T
        kt_ref[:, count:] = rows_of(other_ref, 1).T
        gk_ref[...] = jnp.zeros_like(gk_ref)
        gv_ref[...] = jnp.zeros_like(gv_ref)

    q = mine_ref[pl.ds(step * (TILE // HALF), TILE // HALF), 0].reshape(TILE, HEAD)
    grad = grad_ref[...].reshape(TILE, HEAD)
    out = out_ref[:, :HALF].reshape(TILE, HEAD)
    delta = jnp.sum((grad.astype(F32) * out.astype(F32)).T, axis=0, keepdims=True)
    lse = lse_ref[...]
    gq = jnp.zeros((HEAD, TILE), F32)
    for part, ref in enumerate((mine_ref, other_ref)):
        span = slice(part * count, (part + 1) * count)
        probs = jnp.exp2(dot_nt(rows_of(ref, 1), q) * SCALE2 - lse)
        slope = (probs * (dot_nt(rows_of(ref, 2), grad) - delta)).astype(BF)
        gv_ref[span] += dot(probs.astype(BF), grad)
        gk_ref[span] += dot(slope, q)
        gq = gq + dot(kt_ref[:, span], slope)
    gq_ref[...] = (gq * SCALE).T.astype(BF).reshape(TILE // HALF, HALF, HEAD)

    @pl.when(step == pl.num_programs(0) - 1)
    def _():
        own_ref[:, 0] = (gk_ref[:count] * SCALE).astype(BF).reshape(16, HALF, HEAD)
        own_ref[:, 1] = gv_ref[:count].astype(BF).reshape(16, HALF, HEAD)
        far_ref[:, 0] = (gk_ref[count:] * SCALE).astype(BF).reshape(16, HALF, HEAD)
        far_ref[:, 1] = gv_ref[count:].astype(BF).reshape(16, HALF, HEAD)


def attention_backward(mine, other, out, grad, lse):
    whole = pl.BlockSpec((16, 3, HALF, HEAD), lambda i: (0, 0, 0, 0))
    part = pl.BlockSpec((TILE // HALF, HALF, HEAD), lambda i: (i, 0, 0))
    wide = pl.BlockSpec((TILE // HALF, HALF + EDGE, HEAD), lambda i: (i, 0, 0))
    both = pl.BlockSpec((16, 2, HALF, HEAD), lambda i: (0, 0, 0, 0))
    return pl.pallas_call(
        backward_kernel,
        grid=(16 * HALF // TILE,),
        out_shape=[
            shaped((16, HALF, HEAD)),
            shaped((16, 2, HALF, HEAD)),
            shaped((16, 2, HALF, HEAD)),
        ],
        in_specs=[whole, whole, wide, part, pl.BlockSpec((1, TILE), lambda i: (0, i))],
        out_specs=[part, both, both],
        scratch_shapes=[
            pltpu.VMEM((HEAD, 32 * HALF), BF),
            pltpu.VMEM((32 * HALF, HEAD), F32),
            pltpu.VMEM((32 * HALF, HEAD), F32),
        ],
        compiler_params=params(),
        cost_estimate=cost(10 * 1024 * 2048 * 256, 6 * 1024 * 1024),
    )(mine, other, out, grad, lse)


def row_index(shape):
    return lax.broadcasted_iota(jnp.int32, shape, 0)


def earlier(block):
    return pltpu.roll(block, 1, 0)


def later(block):
    return pltpu.roll(block, block.shape[0] - 1, 0)


def lanes(core, width):
    return pl.ds(pl.multiple_of(core * width, 128), width)


def offset(start, by, width):
    return pl.ds(pl.multiple_of(start + by * width, 128), width)


def middle_kernel(at_ref, att_ref, att_far, res_ref, cot_ref, lo_ref, hi_ref, skip_ref, w_own, w_far, *refs):
    c_own, c_far = refs[:4], refs[4:8]
    dec_ref, att_out, mixed_ref, g_keep, g_send, gm_ref, gm_keep, gm_send, gatt_keep, gatt_send = refs[8:18]
    acc_ref, y_ref, m_ref, g_ref = refs[18:]
    core, x, slab = at_ref[0], at_ref[1], at_ref[2]
    inside = slice(EDGE, EDGE + TOK)

    low = high = None
    for h in range(HEADS):
        mine, other = att_ref[h], att_far[h]
        even = jnp.where(core == 0, mine, other)
        odd = jnp.where(core == 0, other, mine)
        att_out[0, h] = even[:HALF]
        att_out[1, h] = odd[:HALF]
        block = jnp.concatenate([odd[HALF:], even[:HALF], odd[:HALF], even[HALF:]], axis=0)
        a = dot(block, w_own[h * HEAD : (h + 1) * HEAD])
        b = dot(block, w_far[h * HEAD : (h + 1) * HEAD])
        low, high = (a, b) if low is None else (low + a, high + b)
    acc_ref[:, lanes(core, WCOLS)] = low
    acc_ref[:, lanes(1 - core, WCOLS)] = high
    res = jnp.concatenate([lo_ref[:, :WIDTH], res_ref[...], hi_ref[:, :WIDTH]], axis=0)
    mixed = acc_ref[...] + res.astype(F32)
    row = row_index(mixed.shape)
    outside = ((row < EDGE) & (slab == 0)) | ((row >= EDGE + TOK) & (slab == 15))
    m_ref[...] = jnp.where(outside, 0.0, mixed).astype(BF)
    mixed_ref[...] = m_ref[inside]

    for k in range(4):
        by = lax.rem(x + k, 4)
        y_ref[:, offset(core * CCOLS, by, CX)] = dot(m_ref[...], c_own[k][...])
        y_ref[:, offset((1 - core) * CCOLS, by, CX)] = dot(m_ref[...], c_far[k][...])
    y0, y1, y2, y3, y4 = (y_ref[:, t * CH : (t + 1) * CH] for t in range(TAPS))
    even = y2 + y3 + earlier(y0 + y1) + later(y4)
    odd = y1 + y2 + earlier(y0) + later(y3 + y4)
    cot = jnp.concatenate([lo_ref[:, WIDTH:], cot_ref[...], hi_ref[:, WIDTH:]], axis=0)
    grads = []
    for j, pre in enumerate((even, odd)):
        span = slice(j * CH, (j + 1) * CH)
        tanh = jnp.tanh(ROOT * (pre + CUBIC * pre * pre * pre))
        act = 0.5 * pre * (1.0 + tanh)
        slope = 0.5 * (1.0 + tanh) + 0.5 * pre * (1.0 - tanh * tanh) * ROOT * (
            1.0 + 3.0 * CUBIC * pre * pre
        )
        dec_ref[:, span] = (act[inside] + skip_ref[:, span].astype(F32)).astype(BF)
        grads.append((cot[:, span].astype(F32) * slope).astype(BF).astype(F32))

    e, o = grads
    sums = (later(e) + later(o), o + later(e), e + o, earlier(o) + e, earlier(e) + earlier(o))
    for t, block in enumerate(sums):
        g_ref[:, t * CH : (t + 1) * CH] = block[inside].astype(BF)
    g_ref[:, TAPS * CH :] = jnp.zeros((TOK, 2 * CCOLS - TAPS * CH), BF)
    g_keep[...] = g_ref[:, lanes(core, CCOLS)]
    g_send[...] = g_ref[:, lanes(1 - core, CCOLS)]
    gm = jnp.zeros((TOK, WIDTH), F32)
    for k in range(4):
        lanes_k = offset(0, lax.rem(x + k, 4), CX)
        gm = gm + dot_nt(g_keep[:, lanes_k], c_own[k][...]) + dot_nt(g_send[:, lanes_k], c_far[k][...])
    gm_ref[...] = gm.astype(BF)
    gm_keep[...] = gm_ref[:, lanes(core, WCOLS)]
    gm_send[...] = gm_ref[:, lanes(1 - core, WCOLS)]
    for h in range(HEADS):
        rows = slice(h * HEAD, (h + 1) * HEAD)
        block = dot_nt(gm_keep[...], w_own[rows]) + dot_nt(gm_send[...], w_far[rows])
        gatt_keep[h] = jnp.where(core == 0, block[:HALF], block[HALF:]).astype(BF)
        gatt_send[h] = jnp.where(core == 0, block[HALF:], block[:HALF]).astype(BF)


def middle(at, att, att_far, residual, cotangent, edges, skip, weights):
    rows = TOK + 2 * EDGE
    return pl.pallas_call(
        middle_kernel,
        out_shape=[
            shaped((TOK, 2 * CH)),
            shaped((2, HEADS, HALF, HEAD)),
            shaped((TOK, WIDTH)),
            shaped((TOK, CCOLS)),
            shaped((TOK, CCOLS)),
            shaped((TOK, WIDTH)),
            shaped((TOK, WCOLS)),
            shaped((TOK, WCOLS)),
            shaped((HEADS, HALF, HEAD)),
            shaped((HEADS, HALF, HEAD)),
        ],
        in_specs=[SMEM] + [VMEM] * (7 + len(weights)),
        out_specs=[VMEM] * 10,
        scratch_shapes=[
            pltpu.VMEM((rows, WIDTH), F32),
            pltpu.VMEM((rows, 2 * CCOLS), F32),
            pltpu.VMEM((rows, WIDTH), BF),
            pltpu.VMEM((TOK, 2 * CCOLS), BF),
        ],
        compiler_params=params(),
        cost_estimate=cost(8 * rows * WIDTH * 3584, WIDTH * 3584 * 2),
    )(at, att, att_far, residual, cotangent, *edges, skip, *weights)


def terms_kernel(a_ref, a2_ref, m_ref, m2_ref, gm_ref, gm2_ref, g_ref, g2_ref, out_ref, gm_both, g_both):
    step = pl.program_id(0)

    @pl.when(step == 0)
    def _():
        gm_both[:TOK] = gm_ref[...]
        gm_both[TOK:] = gm2_ref[...]
        g_both[:TOK] = g_ref[...]
        g_both[TOK:] = g2_ref[...]

    def store(block, span):
        for x in range(4):
            rows = [block[z * 96 + x * 24 : z * 96 + (x + 1) * 24] for z in range(4)]
            out_ref[x, :, span] = jnp.concatenate(rows, axis=0).astype(BF)

    heads = []
    for j in range(2):
        rows = [r[:, 2 * step + j].reshape(TOK, HEAD) for r in (a_ref, a2_ref)]
        heads.append(jnp.concatenate(rows, axis=0).T)
    store(dot(jnp.concatenate(heads, axis=0), gm_both[...]), slice(0, WCOLS))
    turned = jnp.concatenate([m_ref[...], m2_ref[...]], axis=0).T
    store(dot(turned, g_both[...]), slice(WCOLS, WCOLS + CCOLS))


def weight_terms(att, att2, mixed, mixed2, gm, gm2, g, g2):
    heads = pl.BlockSpec((2, HEADS, HALF, HEAD), lambda i: (0, 0, 0, 0))
    cols = pl.BlockSpec((TOK, 2 * HEAD), lambda i: (0, i))
    gms = pl.BlockSpec((TOK, WCOLS), lambda i: (0, 0))
    gs = pl.BlockSpec((TOK, CCOLS), lambda i: (0, 0))
    columns = WCOLS + CCOLS
    return pl.pallas_call(
        terms_kernel,
        grid=(4,),
        out_shape=shaped((4, 16 * 24, columns)),
        in_specs=[heads, heads, cols, cols, gms, gms, gs, gs],
        out_specs=pl.BlockSpec((4, 4 * 24, columns), lambda i: (0, i, 0)),
        scratch_shapes=[pltpu.VMEM((2 * TOK, WCOLS), BF), pltpu.VMEM((2 * TOK, CCOLS), BF)],
        compiler_params=params(),
        cost_estimate=cost(4 * TOK * WIDTH * columns, WIDTH * columns * 2),
    )(att, att2, mixed, mixed2, gm, gm2, g, g2)


def place_kernel(at_ref, *refs):
    out_ref = refs[-1]
    for k, ref in enumerate(refs[:-1]):
        count = ref.shape[0]
        spot = lax.rem(at_ref[0] + k, 4)
        out_ref[pl.ds(pl.multiple_of(spot * count, 16), count)] = ref[...]


def place(at, pieces):
    rows, columns = pieces[0].shape
    return pl.pallas_call(
        place_kernel,
        out_shape=shaped((4 * rows, columns)),
        in_specs=[SMEM] + [VMEM] * 4,
        out_specs=VMEM,
        compiler_params=params(),
        cost_estimate=cost(0, 16 * rows * columns),
    )(at[None], *pieces)


def finish_kernel(at_ref, *refs):
    pieces = refs[:4]
    out_ref, conv_ref, scratch = refs[4:]
    core, x = at_ref[0], at_ref[1]
    far = 1 - core
    columns = WCOLS + CCOLS
    for k, ref in enumerate(pieces):
        rows = pl.ds(pl.multiple_of(lax.rem(x + k, 4) * 24, 8), 24)
        block = ref[...].astype(F32)
        out_ref[rows, lanes(core, WCOLS)] = block[:, :WCOLS]
        out_ref[rows, lanes(far, WCOLS)] = block[:, columns : columns + WCOLS]
        scratch[:, lanes(core, CCOLS)] = block[:, WCOLS:columns]
        scratch[:, lanes(far, CCOLS)] = block[:, columns + WCOLS :]
        for t in range(TAPS):
            conv_ref[t, rows] = scratch[:, t * CH : (t + 1) * CH]


def finish(at, pieces):
    return pl.pallas_call(
        finish_kernel,
        out_shape=[shaped((96, WIDTH), F32), shaped((TAPS, 96, CH), F32)],
        in_specs=[SMEM] + [VMEM] * 4,
        out_specs=[VMEM] * 2,
        scratch_shapes=[pltpu.VMEM((24, 2 * CCOLS), F32)],
        compiler_params=params(),
        cost_estimate=cost(0, 96 * 3584 * 6),
    )(at, *pieces)


def tied(block, *others):
    return lax.optimization_barrier((block, *others))[0]


def shifted(block, axis, by):
    return lax.ppermute(block, axis, [((i + by) % 4, i) for i in range(4)])


def around(block, axis):
    return [block] + [shifted(block, axis, by) for by in (1, 2, 3)]


def sent_to(parts, axis):
    return [parts[0]] + [shifted(parts[k], axis, 4 - k) for k in (1, 2, 3)]


def parts_of(blocks, axis, dim=0):
    at = lax.axis_index(axis)
    return [
        lax.dynamic_index_in_dim(blocks, lax.rem(at + k, 4), dim, keepdims=False) for k in range(4)
    ]


def summed(blocks):
    total = blocks[0].astype(F32)
    for block in blocks[1:]:
        total = total + block.astype(F32)
    return total.astype(BF)


def swap(block, axis="core"):
    return lax.ppermute(block, axis, [(0, 1), (1, 0)])


def exchange(block, axis):
    return lax.all_to_all(block, axis, split_axis=0, concat_axis=0, tiled=True)


def neighbours(to_next, to_prev):
    up = [(i, i + 1) for i in range(15)]
    return (
        lax.ppermute(to_next, SEQ, up),
        lax.ppermute(to_prev, SEQ, [(b, a) for a, b in up]),
    )


def body(queries, keys, values, residual, out_weight, conv_weight, skip, cotangent):
    core, x, y, zh = (lax.axis_index(a).astype(jnp.int32) for a in ("core", "x", "y", "zh"))
    at = jnp.stack([core, x, 4 * y + zh])
    residual, cotangent = residual[0], cotangent[0].reshape(TOK, 2 * CH)
    edges = [
        jnp.concatenate([block[rows] for block in (residual, cotangent)], axis=1)
        for rows in (slice(-EDGE, None), slice(0, EDGE))
    ]

    conv_rows = jnp.pad(
        conv_weight.transpose(1, 0, 2).reshape(-1, TAPS * CH), ((0, 0), (0, 2 * CCOLS - TAPS * CH))
    )
    c_part = lax.dynamic_slice_in_dim(conv_rows, core * CCOLS + x * CX, CX, axis=1)
    c_part = place(zh, around(c_part, "zh"))
    w_own = lax.dynamic_slice_in_dim(out_weight, core * WCOLS, WCOLS, axis=1)
    w_own = lax.all_gather(w_own, SEQ, axis=0, tiled=True)

    packed = exchange(pack(queries[0], keys[0], values[0]), "core")
    mine = exchange(tied(packed, c_part).reshape(16, 3, HALF, HEAD), SEQ)
    c_all = place(y, around(c_part, "y"))
    c_own = around(c_all, "x")
    edges = neighbours(*edges)
    skip = skip[0].reshape(TOK, 2 * CH)
    mine = tied(mine, c_own[1], c_own[3], *edges, skip, cotangent)
    other = swap(mine)
    out, lse = attention_forward(at, mine, other)
    back = exchange(out, SEQ)
    w_own = tied(w_own, out)
    w_far = swap(w_own)
    c_far = [swap(tied(piece, out)) for piece in c_own]
    att = lax.dynamic_slice_in_dim(back, core * HEADS, HEADS, axis=0)
    att_far = swap(lax.dynamic_slice_in_dim(back, (1 - core) * HEADS, HEADS, axis=0))

    weights = [w_own, w_far, *c_own, *c_far]
    decoded, att, mixed, g_keep, g_send, gm, gm_keep, gm_send, gatt, gatt_send = middle(
        at, att, att_far, residual, cotangent, edges, skip, weights
    )

    gatt = join(at, gatt, swap(gatt_send))

    columns = WCOLS + CCOLS
    part = weight_terms(
        att, swap(att), mixed, swap(mixed), gm_keep, swap(gm_send), g_keep, swap(g_send)
    )
    part = lax.psum_scatter(part.reshape(-1, columns), "x", scatter_dimension=0, tiled=True)

    grad = exchange(gatt, SEQ)
    gq, own, far = attention_backward(mine, other, out, grad, lse)
    both = (own.astype(F32) + swap(far).astype(F32)).astype(BF)
    both = jnp.concatenate([gq[:, None], both], axis=1)
    part = parts_of(tied(part, both).reshape(4, 96, columns), "y")
    part = summed(sent_to(part, "y")).reshape(4, 24, columns)
    part = sent_to(parts_of(part, "zh"), "zh")
    back = exchange(both, SEQ)

    far = swap(lax.dynamic_slice_in_dim(back, (1 - core) * HEADS, HEADS, axis=0))
    keep = lax.dynamic_slice_in_dim(back, core * HEADS, HEADS, axis=0)
    gq, gk, gv = unpack(at, keep, far)
    part = summed([tied(b, gq) for b in part])
    across = [lax.ppermute(part, ("zl", "core"), [(i, i ^ by) for i in range(4)]) for by in (2, 1, 3)]
    sums = [summed([part, across[0]]), summed(across[1:])]
    pieces = around(jnp.concatenate(sums, axis=1), "x")
    grad_out, grad_conv = finish(jnp.stack([core, x]), pieces)
    return (
        decoded.reshape(1, 2 * TOK, CH),
        gq[None],
        gk[None],
        gv[None],
        gm[None],
        grad_out,
        grad_conv,
    )


def solution(mesh):
    grid = Mesh(mesh.devices.reshape(2, 4, 2, 4, 4), ("zl", "x", "core", "y", "zh"))
    dp = ("zl", "x", "core")
    tokens = P(dp, SEQ, None)
    in_specs = (tokens, tokens, tokens, tokens, P(SEQ, None), P(None, SEQ, None), tokens, tokens)
    out_specs = (tokens, tokens, tokens, tokens, tokens, P(SEQ, None), P(None, SEQ, None))
    return jax.shard_map(body, mesh=grid, in_specs=in_specs, out_specs=out_specs, check_vma=False)
```

```python
import math

import jax
import jax.numpy as jnp
from jax import lax
from jax.experimental import pallas as pl
from jax.experimental.pallas import tpu as pltpu
from jax.sharding import Mesh
from jax.sharding import PartitionSpec as P

HEADS = 8
HEAD = 192
WIDTH = 1536
TOK = 128
HALF = 64
EDGE = 16
CH = 384
TAPS = 5
WCOLS = 768
CX = 256
CCOLS = 1024
SEQ = ("y", "zh")
ROOT = math.sqrt(2.0 / math.pi)
CUBIC = 0.044715
SCALE = HEAD ** (-0.5)
SCALE2 = SCALE * math.log2(math.e)
BF = jnp.bfloat16
F32 = jnp.float32
VMEM = pl.BlockSpec(memory_space=pltpu.VMEM)
SMEM = pl.BlockSpec(memory_space=pltpu.SMEM)


def params():
    return pltpu.CompilerParams(vmem_limit_bytes=56 * 1024 * 1024)


def cost(flops, nbytes):
    return pl.CostEstimate(flops=int(flops) // 50, bytes_accessed=int(nbytes) // 50, transcendentals=0)


def shaped(shape, dtype=BF):
    return jax.ShapeDtypeStruct(shape, dtype)


def dot(a, b):
    return jnp.dot(a, b, preferred_element_type=F32)


def dot_nt(a, b):
    return lax.dot_general(a, b, (((1,), (1,)), ((), ())), preferred_element_type=F32)


def pack_kernel(q_ref, k_ref, v_ref, o_ref):
    for j, ref in enumerate((q_ref, k_ref, v_ref)):
        for half in range(2):
            for h in range(HEADS):
                o_ref[half, h, j] = ref[half * HALF : (half + 1) * HALF, h * HEAD : (h + 1) * HEAD]


def pack(q, k, v):
    return pl.pallas_call(
        pack_kernel,
        out_shape=shaped((2, HEADS, 3, HALF, HEAD)),
        in_specs=[VMEM] * 3,
        out_specs=VMEM,
        compiler_params=params(),
        cost_estimate=cost(0, 3 * 2 * TOK * WIDTH * 2),
    )(q, k, v)


def unpack_kernel(at_ref, keep_ref, far_ref, q_ref, k_ref, v_ref):
    core = at_ref[0]
    for j, ref in enumerate((q_ref, k_ref, v_ref)):
        for h in range(HEADS):
            lanes_h = slice(h * HEAD, (h + 1) * HEAD)
            ref[pl.ds(pl.multiple_of(core * HALF, HALF), HALF), lanes_h] = keep_ref[h, j]
            ref[pl.ds(pl.multiple_of((1 - core) * HALF, HALF), HALF), lanes_h] = far_ref[h, j]


def unpack(at, keep, far):
    return pl.pallas_call(
        unpack_kernel,
        out_shape=[shaped((TOK, WIDTH))] * 3,
        in_specs=[SMEM] + [VMEM] * 2,
        out_specs=[VMEM] * 3,
        compiler_params=params(),
        cost_estimate=cost(0, 3 * 2 * TOK * WIDTH * 2),
    )(at, keep, far)


def join_kernel(at_ref, own_ref, far_ref, out_ref):
    core = at_ref[0]
    out_ref[pl.ds(core * HEADS, HEADS)] = own_ref[...]
    out_ref[pl.ds((1 - core) * HEADS, HEADS)] = far_ref[...]


def join(at, own, far):
    return pl.pallas_call(
        join_kernel,
        out_shape=shaped((2 * own.shape[0], *own.shape[1:])),
        in_specs=[SMEM] + [VMEM] * 2,
        out_specs=VMEM,
        compiler_params=params(),
        cost_estimate=cost(0, own.size * 8),
    )(at, own, far)


def rows_of(ref, j):
    return ref[:, j].reshape(16 * HALF, HEAD)


def forward_kernel(at_ref, mine_ref, other_ref, out_ref, lse_ref):
    core = at_ref[0]
    q = rows_of(mine_ref, 0)
    s_a = dot_nt(rows_of(mine_ref, 1), q)
    s_b = dot_nt(rows_of(other_ref, 1), q)
    peak = jnp.maximum(jnp.max(s_a, axis=0, keepdims=True), jnp.max(s_b, axis=0, keepdims=True))
    peak = peak * SCALE2
    e_a = jnp.exp2(s_a * SCALE2 - peak)
    e_b = jnp.exp2(s_b * SCALE2 - peak)
    total = jnp.sum(e_a, axis=0, keepdims=True) + jnp.sum(e_b, axis=0, keepdims=True)
    out = dot(rows_of(mine_ref, 2).T, e_a.astype(BF)) + dot(rows_of(other_ref, 2).T, e_b.astype(BF))
    out = (out / total).T
    for slab in range(16):
        rows = out[slab * HALF : (slab + 1) * HALF]
        out_ref[slab, :HALF] = rows.astype(BF)
        edge = jnp.where(core == 0, rows[:EDGE], rows[HALF - EDGE :])
        out_ref[lax.rem(slab + 15 + 2 * core, 16), HALF:] = edge.astype(BF)
    lse_ref[...] = peak + jnp.log2(total)


def attention_forward(at, mine, other):
    return pl.pallas_call(
        forward_kernel,
        out_shape=[shaped((16, HALF + EDGE, HEAD)), shaped((1, 16 * HALF), F32)],
        in_specs=[SMEM] + [VMEM] * 2,
        out_specs=[VMEM] * 2,
        compiler_params=params(),
        cost_estimate=cost(4 * 1024 * 2048 * 256, 3 * 1024 * 1024),
    )(at, mine, other)


def backward_kernel(mine_ref, other_ref, out_ref, grad_ref, lse_ref, gq_ref, own_ref, far_ref):
    q = rows_of(mine_ref, 0)
    grad = grad_ref[...].reshape(16 * HALF, HEAD)
    out = out_ref[:, :HALF].reshape(16 * HALF, HEAD)
    delta = jnp.sum((grad.astype(F32) * out.astype(F32)).T, axis=0, keepdims=True)
    lse = lse_ref[...]
    gq = jnp.zeros((HEAD, 16 * HALF), F32)
    for ref, to_ref in ((mine_ref, own_ref), (other_ref, far_ref)):
        keys = rows_of(ref, 1)
        probs = jnp.exp2(dot_nt(keys, q) * SCALE2 - lse)
        slope = (probs * (dot_nt(rows_of(ref, 2), grad) - delta)).astype(BF)
        to_ref[:, 1] = dot(probs.astype(BF), grad).astype(BF).reshape(16, HALF, HEAD)
        to_ref[:, 0] = (dot(slope, q) * SCALE).astype(BF).reshape(16, HALF, HEAD)
        gq = gq + dot(keys.T, slope)
    gq_ref[...] = (gq * SCALE).T.astype(BF).reshape(16, HALF, HEAD)


def attention_backward(mine, other, out, grad, lse):
    return pl.pallas_call(
        backward_kernel,
        out_shape=[
            shaped((16, HALF, HEAD)),
            shaped((16, 2, HALF, HEAD)),
            shaped((16, 2, HALF, HEAD)),
        ],
        in_specs=[VMEM] * 5,
        out_specs=[VMEM] * 3,
        compiler_params=params(),
        cost_estimate=cost(10 * 1024 * 2048 * 256, 6 * 1024 * 1024),
    )(mine, other, out, grad, lse)


def row_index(shape):
    return lax.broadcasted_iota(jnp.int32, shape, 0)


def earlier(block):
    return pltpu.roll(block, 1, 0)


def later(block):
    return pltpu.roll(block, block.shape[0] - 1, 0)


def lanes(core, width):
    return pl.ds(pl.multiple_of(core * width, 128), width)


def offset(start, by, width):
    return pl.ds(pl.multiple_of(start + by * width, 128), width)


def middle_kernel(at_ref, att_ref, att_far, res_ref, cot_ref, lo_ref, hi_ref, skip_ref, w_own, w_far, *refs):
    c_own, c_far = refs[:4], refs[4:8]
    dec_ref, att_out, mixed_ref, g_keep, g_send, gm_ref, gm_keep, gm_send, gatt_keep, gatt_send = refs[8:18]
    acc_ref, y_ref, m_ref, g_ref = refs[18:]
    core, x, slab = at_ref[0], at_ref[1], at_ref[2]
    inside = slice(EDGE, EDGE + TOK)

    low = high = None
    for h in range(HEADS):
        mine, other = att_ref[h], att_far[h]
        even = jnp.where(core == 0, mine, other)
        odd = jnp.where(core == 0, other, mine)
        att_out[0, h] = even[:HALF]
        att_out[1, h] = odd[:HALF]
        block = jnp.concatenate([odd[HALF:], even[:HALF], odd[:HALF], even[HALF:]], axis=0)
        a = dot(block, w_own[h * HEAD : (h + 1) * HEAD])
        b = dot(block, w_far[h * HEAD : (h + 1) * HEAD])
        low, high = (a, b) if low is None else (low + a, high + b)
    acc_ref[:, lanes(core, WCOLS)] = low
    acc_ref[:, lanes(1 - core, WCOLS)] = high
    res = jnp.concatenate([lo_ref[:, :WIDTH], res_ref[...], hi_ref[:, :WIDTH]], axis=0)
    mixed = acc_ref[...] + res.astype(F32)
    row = row_index(mixed.shape)
    outside = ((row < EDGE) & (slab == 0)) | ((row >= EDGE + TOK) & (slab == 15))
    m_ref[...] = jnp.where(outside, 0.0, mixed).astype(BF)
    mixed_ref[...] = m_ref[inside]

    for k in range(4):
        by = lax.rem(x + k, 4)
        y_ref[:, offset(core * CCOLS, by, CX)] = dot(m_ref[...], c_own[k][...])
        y_ref[:, offset((1 - core) * CCOLS, by, CX)] = dot(m_ref[...], c_far[k][...])
    y0, y1, y2, y3, y4 = (y_ref[:, t * CH : (t + 1) * CH] for t in range(TAPS))
    even = y2 + y3 + earlier(y0 + y1) + later(y4)
    odd = y1 + y2 + earlier(y0) + later(y3 + y4)
    cot = jnp.concatenate([lo_ref[:, WIDTH:], cot_ref[...], hi_ref[:, WIDTH:]], axis=0)
    grads = []
    for j, pre in enumerate((even, odd)):
        span = slice(j * CH, (j + 1) * CH)
        tanh = jnp.tanh(ROOT * (pre + CUBIC * pre * pre * pre))
        act = 0.5 * pre * (1.0 + tanh)
        slope = 0.5 * (1.0 + tanh) + 0.5 * pre * (1.0 - tanh * tanh) * ROOT * (
            1.0 + 3.0 * CUBIC * pre * pre
        )
        dec_ref[:, span] = (act[inside] + skip_ref[:, span].astype(F32)).astype(BF)
        grads.append((cot[:, span].astype(F32) * slope).astype(BF).astype(F32))

    e, o = grads
    sums = (later(e) + later(o), o + later(e), e + o, earlier(o) + e, earlier(e) + earlier(o))
    for t, block in enumerate(sums):
        g_ref[:, t * CH : (t + 1) * CH] = block[inside].astype(BF)
    g_ref[:, TAPS * CH :] = jnp.zeros((TOK, 2 * CCOLS - TAPS * CH), BF)
    g_keep[...] = g_ref[:, lanes(core, CCOLS)]
    g_send[...] = g_ref[:, lanes(1 - core, CCOLS)]
    gm = jnp.zeros((TOK, WIDTH), F32)
    for k in range(4):
        lanes_k = offset(0, lax.rem(x + k, 4), CX)
        gm = gm + dot_nt(g_keep[:, lanes_k], c_own[k][...]) + dot_nt(g_send[:, lanes_k], c_far[k][...])
    gm_ref[...] = gm.astype(BF)
    gm_keep[...] = gm_ref[:, lanes(core, WCOLS)]
    gm_send[...] = gm_ref[:, lanes(1 - core, WCOLS)]
    for h in range(HEADS):
        rows = slice(h * HEAD, (h + 1) * HEAD)
        block = dot_nt(gm_keep[...], w_own[rows]) + dot_nt(gm_send[...], w_far[rows])
        gatt_keep[h] = jnp.where(core == 0, block[:HALF], block[HALF:]).astype(BF)
        gatt_send[h] = jnp.where(core == 0, block[HALF:], block[:HALF]).astype(BF)


def middle(at, att, att_far, residual, cotangent, edges, skip, weights):
    rows = TOK + 2 * EDGE
    return pl.pallas_call(
        middle_kernel,
        out_shape=[
            shaped((TOK, 2 * CH)),
            shaped((2, HEADS, HALF, HEAD)),
            shaped((TOK, WIDTH)),
            shaped((TOK, CCOLS)),
            shaped((TOK, CCOLS)),
            shaped((TOK, WIDTH)),
            shaped((TOK, WCOLS)),
            shaped((TOK, WCOLS)),
            shaped((HEADS, HALF, HEAD)),
            shaped((HEADS, HALF, HEAD)),
        ],
        in_specs=[SMEM] + [VMEM] * (7 + len(weights)),
        out_specs=[VMEM] * 10,
        scratch_shapes=[
            pltpu.VMEM((rows, WIDTH), F32),
            pltpu.VMEM((rows, 2 * CCOLS), F32),
            pltpu.VMEM((rows, WIDTH), BF),
            pltpu.VMEM((TOK, 2 * CCOLS), BF),
        ],
        compiler_params=params(),
        cost_estimate=cost(8 * rows * WIDTH * 3584, WIDTH * 3584 * 2),
    )(at, att, att_far, residual, cotangent, *edges, skip, *weights)


def terms_kernel(a_ref, a2_ref, m_ref, m2_ref, gm_ref, gm2_ref, g_ref, g2_ref, out_ref, gm_both, g_both):
    step = pl.program_id(0)

    @pl.when(step == 0)
    def _():
        gm_both[:TOK] = gm_ref[...]
        gm_both[TOK:] = gm2_ref[...]
        g_both[:TOK] = g_ref[...]
        g_both[TOK:] = g2_ref[...]

    def store(block, span):
        for x in range(4):
            rows = [block[z * 96 + x * 24 : z * 96 + (x + 1) * 24] for z in range(4)]
            out_ref[x, :, span] = jnp.concatenate(rows, axis=0).astype(BF)

    heads = []
    for j in range(2):
        rows = [r[:, 2 * step + j].reshape(TOK, HEAD) for r in (a_ref, a2_ref)]
        heads.append(jnp.concatenate(rows, axis=0).T)
    store(dot(jnp.concatenate(heads, axis=0), gm_both[...]), slice(0, WCOLS))
    turned = jnp.concatenate([m_ref[...], m2_ref[...]], axis=0).T
    store(dot(turned, g_both[...]), slice(WCOLS, WCOLS + CCOLS))


def weight_terms(att, att2, mixed, mixed2, gm, gm2, g, g2):
    heads = pl.BlockSpec((2, HEADS, HALF, HEAD), lambda i: (0, 0, 0, 0))
    cols = pl.BlockSpec((TOK, 2 * HEAD), lambda i: (0, i))
    gms = pl.BlockSpec((TOK, WCOLS), lambda i: (0, 0))
    gs = pl.BlockSpec((TOK, CCOLS), lambda i: (0, 0))
    columns = WCOLS + CCOLS
    return pl.pallas_call(
        terms_kernel,
        grid=(4,),
        out_shape=shaped((4, 16 * 24, columns)),
        in_specs=[heads, heads, cols, cols, gms, gms, gs, gs],
        out_specs=pl.BlockSpec((4, 4 * 24, columns), lambda i: (0, i, 0)),
        scratch_shapes=[pltpu.VMEM((2 * TOK, WCOLS), BF), pltpu.VMEM((2 * TOK, CCOLS), BF)],
        compiler_params=params(),
        cost_estimate=cost(4 * TOK * WIDTH * columns, WIDTH * columns * 2),
    )(att, att2, mixed, mixed2, gm, gm2, g, g2)


def place_kernel(at_ref, *refs):
    out_ref = refs[-1]
    for k, ref in enumerate(refs[:-1]):
        count = ref.shape[0]
        spot = lax.rem(at_ref[0] + k, 4)
        out_ref[pl.ds(pl.multiple_of(spot * count, 16), count)] = ref[...]


def place(at, pieces):
    rows, columns = pieces[0].shape
    return pl.pallas_call(
        place_kernel,
        out_shape=shaped((4 * rows, columns)),
        in_specs=[SMEM] + [VMEM] * 4,
        out_specs=VMEM,
        compiler_params=params(),
        cost_estimate=cost(0, 16 * rows * columns),
    )(at[None], *pieces)


def finish_kernel(at_ref, *refs):
    pieces = refs[:4]
    out_ref, conv_ref, scratch = refs[4:]
    core, x = at_ref[0], at_ref[1]
    far = 1 - core
    columns = WCOLS + CCOLS
    for k, ref in enumerate(pieces):
        rows = pl.ds(pl.multiple_of(lax.rem(x + k, 4) * 24, 8), 24)
        block = ref[...].astype(F32)
        out_ref[rows, lanes(core, WCOLS)] = block[:, :WCOLS]
        out_ref[rows, lanes(far, WCOLS)] = block[:, columns : columns + WCOLS]
        scratch[:, lanes(core, CCOLS)] = block[:, WCOLS:columns]
        scratch[:, lanes(far, CCOLS)] = block[:, columns + WCOLS :]
        for t in range(TAPS):
            conv_ref[t, rows] = scratch[:, t * CH : (t + 1) * CH]


def finish(at, pieces):
    return pl.pallas_call(
        finish_kernel,
        out_shape=[shaped((96, WIDTH), F32), shaped((TAPS, 96, CH), F32)],
        in_specs=[SMEM] + [VMEM] * 4,
        out_specs=[VMEM] * 2,
        scratch_shapes=[pltpu.VMEM((24, 2 * CCOLS), F32)],
        compiler_params=params(),
        cost_estimate=cost(0, 96 * 3584 * 6),
    )(at, *pieces)


def tied(block, *others):
    return lax.optimization_barrier((block, *others))[0]


def shifted(block, axis, by):
    return lax.ppermute(block, axis, [((i + by) % 4, i) for i in range(4)])


def around(block, axis):
    return [block] + [shifted(block, axis, by) for by in (1, 2, 3)]


def sent_to(parts, axis):
    return [parts[0]] + [shifted(parts[k], axis, 4 - k) for k in (1, 2, 3)]


def parts_of(blocks, axis, dim=0):
    at = lax.axis_index(axis)
    return [
        lax.dynamic_index_in_dim(blocks, lax.rem(at + k, 4), dim, keepdims=False) for k in range(4)
    ]


def summed(blocks):
    total = blocks[0].astype(F32)
    for block in blocks[1:]:
        total = total + block.astype(F32)
    return total.astype(BF)


def swap(block, axis="core"):
    return lax.ppermute(block, axis, [(0, 1), (1, 0)])


def exchange(block, axis):
    return lax.all_to_all(block, axis, split_axis=0, concat_axis=0, tiled=True)


def neighbours(to_next, to_prev):
    up = [(i, i + 1) for i in range(15)]
    return (
        lax.ppermute(to_next, SEQ, up),
        lax.ppermute(to_prev, SEQ, [(b, a) for a, b in up]),
    )


def body(queries, keys, values, residual, out_weight, conv_weight, skip, cotangent):
    core, x, y, zh = (lax.axis_index(a).astype(jnp.int32) for a in ("core", "x", "y", "zh"))
    at = jnp.stack([core, x, 4 * y + zh])
    residual, cotangent = residual[0], cotangent[0].reshape(TOK, 2 * CH)
    edges = [
        jnp.concatenate([block[rows] for block in (residual, cotangent)], axis=1)
        for rows in (slice(-EDGE, None), slice(0, EDGE))
    ]

    conv_rows = jnp.pad(
        conv_weight.transpose(1, 0, 2).reshape(-1, TAPS * CH), ((0, 0), (0, 2 * CCOLS - TAPS * CH))
    )
    packed = pack(queries[0], keys[0], values[0])
    c_part = lax.dynamic_slice_in_dim(conv_rows, core * CCOLS + x * CX, CX, axis=1)
    c_part = tied(c_part, packed)
    c_part = place(zh, around(c_part, "zh"))
    w_own = lax.dynamic_slice_in_dim(out_weight, core * WCOLS, WCOLS, axis=1)
    w_own = lax.all_gather(w_own, SEQ, axis=0, tiled=True)

    packed = exchange(packed, "core")
    mine = exchange(tied(packed, c_part).reshape(16, 3, HALF, HEAD), SEQ)
    c_all = place(y, around(c_part, "y"))
    c_own = around(c_all, "x")
    edges = neighbours(*edges)
    skip = skip[0].reshape(TOK, 2 * CH)
    mine = tied(mine, c_own[1], c_own[3], *edges, skip, cotangent)
    other = swap(mine)
    out, lse = attention_forward(at, mine, other)
    back = exchange(out, SEQ)
    w_own = tied(w_own, out)
    w_far = swap(w_own)
    c_far = [swap(tied(piece, out)) for piece in c_own]
    att = lax.dynamic_slice_in_dim(back, core * HEADS, HEADS, axis=0)
    att_far = swap(lax.dynamic_slice_in_dim(back, (1 - core) * HEADS, HEADS, axis=0))

    weights = [w_own, w_far, *c_own, *c_far]
    decoded, att, mixed, g_keep, g_send, gm, gm_keep, gm_send, gatt, gatt_send = middle(
        at, att, att_far, residual, cotangent, edges, skip, weights
    )

    gatt = join(at, gatt, swap(gatt_send))

    columns = WCOLS + CCOLS
    part = weight_terms(
        att, swap(att), mixed, swap(mixed), gm_keep, swap(gm_send), g_keep, swap(g_send)
    )
    part = lax.psum_scatter(part.reshape(-1, columns), "x", scatter_dimension=0, tiled=True)

    grad = exchange(gatt, SEQ)
    gq, own, far = attention_backward(mine, other, out, grad, lse)
    both = (own.astype(F32) + swap(far).astype(F32)).astype(BF)
    both = jnp.concatenate([gq[:, None], both], axis=1)
    part = parts_of(tied(part, both).reshape(4, 96, columns), "y")
    part = summed(sent_to(part, "y")).reshape(4, 24, columns)
    part = sent_to(parts_of(part, "zh"), "zh")
    back = exchange(both, SEQ)

    far = swap(lax.dynamic_slice_in_dim(back, (1 - core) * HEADS, HEADS, axis=0))
    keep = lax.dynamic_slice_in_dim(back, core * HEADS, HEADS, axis=0)
    gq, gk, gv = unpack(at, keep, far)
    part = summed([tied(b, gq) for b in part])
    across = [lax.ppermute(part, ("zl", "core"), [(i, i ^ by) for i in range(4)]) for by in (2, 1, 3)]
    sums = [summed([part, across[0]]), summed(across[1:])]
    pieces = around(jnp.concatenate(sums, axis=1), "x")
    grad_out, grad_conv = finish(jnp.stack([core, x]), pieces)
    return (
        decoded.reshape(1, 2 * TOK, CH),
        gq[None],
        gk[None],
        gv[None],
        gm[None],
        grad_out,
        grad_conv,
    )


def solution(mesh):
    grid = Mesh(mesh.devices.reshape(2, 4, 2, 4, 4), ("zl", "x", "core", "y", "zh"))
    dp = ("zl", "x", "core")
    tokens = P(dp, SEQ, None)
    in_specs = (tokens, tokens, tokens, tokens, P(SEQ, None), P(None, SEQ, None), tokens, tokens)
    out_specs = (tokens, tokens, tokens, tokens, tokens, P(SEQ, None), P(None, SEQ, None))
    return jax.shard_map(body, mesh=grid, in_specs=in_specs, out_specs=out_specs, check_vma=False)
```
